256 devices in a mesh: rep: 16 (over z_lo, x, core), ctx: 16 (over z_hi, y).
Axes of the slice: x: 4, y: 4, z: 8 (z_hi: 4, z_lo: 2; z = z_hi * 2 + z_lo), core: 2. Of those that a mesh axis runs over, the one named last changes fastest.
Arguments:
- query_feat: bfloat16 [16, 6144, 512], P('rep', 'ctx'), may hold values from -6 to 6
- key_feat: bfloat16 [16, 6144, 512], P('rep', 'ctx'), may hold values from -6 to 6
- value_feat: bfloat16 [16, 6144, 512], P('rep', 'ctx'), may hold values from -6 to 6
- filter_taps: float32 [6144, 512], P(None, 'ctx'), may hold values from -1.2 to 1.2
- out_cotangent: bfloat16 [16, 6144, 512], P('rep', 'ctx'), may hold values from -6 to 6
Outputs:
- operator_out: bfloat16 [16, 6144, 512], P('rep', 'ctx')
- grad_query: bfloat16 [16, 6144, 512], P('rep', 'ctx')
- grad_key: bfloat16 [16, 6144, 512], P('rep', 'ctx')
- grad_value: bfloat16 [16, 6144, 512], P('rep', 'ctx')
- grad_filter: float32 [6144, 512], P('rep', 'ctx')
The draws below stay inside these ranges and needn't reach their ends.
All inputs are finite; a program needn't handle non-finite values.
Results may differ from the reference program's by a relative error of at most 0.022.
Values may be sent and summed in bfloat16 or wider, within the bound.
A program may use at most 64 MiB of HBM per device.

```python
import math
import jax
import jax.numpy as jnp
from jax import lax

CH = 512
SEQS = 16
SEQUENCE_LENGTH = 6144


def draw_filter_taps(key, part):
    key = jax.random.fold_in(key, 11)
    random_key_list = jax.random.split(key, 5)
    fast_share = 0.5
    position_index = jnp.arange(SEQUENCE_LENGTH, dtype=jnp.float32)[:, None]
    fast_mask = jax.random.uniform(random_key_list[0], (CH,), jnp.float32) < fast_share
    fast_rate = jax.random.uniform(random_key_list[1], (CH,), jnp.float32, 1.0 / 50.0, 1.0 / 30.0)
    slow_rate = math.log(10.0) / SEQUENCE_LENGTH * jax.random.uniform(random_key_list[2], (CH,), jnp.float32, 0.2, 0.6)
    falloff_speed = jnp.where(fast_mask, fast_rate, slow_rate)[None, :]
    spike_locations = jax.random.randint(random_key_list[3], (3,), 0, SEQUENCE_LENGTH).astype(jnp.float32)
    check_succeeded = jnp.sum((position_index > spike_locations[None, :]).astype(jnp.float32), axis=1, keepdims=True)
    spike_amplitude = jnp.power(0.75, check_succeeded)
    random_noise_grid = jnp.clip(jax.random.normal(random_key_list[4], (SEQUENCE_LENGTH, CH), jnp.float32), -4.0, 4.0)
    filter_tap_grid = jnp.sqrt(2.0 * falloff_speed) * jnp.exp(-falloff_speed * position_index) * spike_amplitude * random_noise_grid
    return filter_tap_grid.astype(jnp.float32)


def steps_of(own_key, extent, shards, least, largest):
    def one(position, shards_of):
        heights = jax.random.uniform(jax.random.fold_in(jax.random.fold_in(own_key, 6), position), (shards_of,), jnp.float32, least / len(shards), largest / len(shards))
        return jnp.repeat(jnp.exp(heights), extent[position] // shards_of).reshape((-1,) + (1,) * (len(extent) - position - 1))

    level = one(*shards[0])
    for cut in shards[1:]:
        level = level * one(*cut)
    return level


def noise(key, shape, deviation, bound, cuts=(), held_as=jnp.bfloat16):
    entries = deviation * jax.random.normal(key, shape, jnp.float32)
    if cuts:
        entries = entries * steps_of(key, shape, cuts, -0.22, 0.18)
    return jnp.clip(entries, -bound, bound).astype(held_as)


def setup_inputs(seed: int = 0) -> dict:
    streams_of = jax.random.split(jax.random.key(seed), 6)
    return {
        "query_feat": noise(streams_of[0], (SEQS, SEQUENCE_LENGTH, CH), 1.0, 6.0, ((0, 16), (1, 16))),
        "key_feat": noise(streams_of[1], (SEQS, SEQUENCE_LENGTH, CH), 1.0, 6.0, ((0, 16), (1, 16))),
        "value_feat": noise(streams_of[2], (SEQS, SEQUENCE_LENGTH, CH), 1.0, 6.0, ((0, 16), (1, 16))),
        "filter_taps": draw_filter_taps(jax.random.fold_in(streams_of[5], 71), 0),
        "out_cotangent": noise(streams_of[4], (SEQS, SEQUENCE_LENGTH, CH), 1.0, 6.0, ((0, 16), (1, 16))),
    }


def spectrum(signal):
    return jnp.fft.rfft(signal.astype(jnp.float32), n=2 * SEQUENCE_LENGTH, axis=0)

def inverse(product):
    return jnp.fft.irfft(product, n=2 * SEQUENCE_LENGTH, axis=0)[:SEQUENCE_LENGTH]

def reference(query_feat, key_feat, value_feat, filter_taps, out_cotangent):
    grad_scale = 1.0 / math.sqrt(SEQS * SEQUENCE_LENGTH)
    filter_spec = spectrum(filter_taps)

    def one_sequence(running, pieces):
        query_rows, key_rows, value_rows, cotan_rows = pieces
        gated = (key_rows.astype(jnp.float32) * value_rows.astype(jnp.float32)).astype(jnp.bfloat16)
        back_gate = (cotan_rows.astype(jnp.float32) * query_rows.astype(jnp.float32)).astype(jnp.bfloat16)
        gated_spec = spectrum(gated)
        back_spec = spectrum(back_gate)
        conv_out = inverse(gated_spec * filter_spec).astype(jnp.bfloat16)
        back_conv = inverse(back_spec * jnp.conj(filter_spec)).astype(jnp.bfloat16)
        filter_term = inverse(back_spec * jnp.conj(gated_spec))
        conv_wide = conv_out.astype(jnp.float32)
        back_wide = back_conv.astype(jnp.float32)
        operator_out = (query_rows.astype(jnp.float32) * conv_wide).astype(jnp.bfloat16)
        grad_query = (cotan_rows.astype(jnp.float32) * conv_wide).astype(jnp.bfloat16)
        grad_key = (back_wide * value_rows.astype(jnp.float32)).astype(jnp.bfloat16)
        grad_value = (back_wide * key_rows.astype(jnp.float32)).astype(jnp.bfloat16)
        return (running + filter_term, (operator_out, grad_query, grad_key, grad_value))
    initial = jnp.zeros((SEQUENCE_LENGTH, CH), jnp.float32)
    summed, outputs = lax.scan(one_sequence, initial, (query_feat, key_feat, value_feat, out_cotangent))
    grad_filter = summed * grad_scale
    return (outputs[0], outputs[1], outputs[2], outputs[3], grad_filter)
```

```python
import functools
import math

import jax
import jax.numpy as jnp
import ml_dtypes
import numpy as np
from jax import lax
from jax.experimental import pallas as pl
from jax.experimental.pallas import tpu as pltpu
from jax.sharding import PartitionSpec as P

MESH = pl.DeviceIdType.MESH
F32 = jnp.float32
BF16 = jnp.bfloat16
LANES = 128
HALF = 56
GROUP = 4


def split_table(table):
    high = table.astype(ml_dtypes.bfloat16)
    low = (table - high.astype(np.float64)).astype(ml_dtypes.bfloat16)
    return high, low


def wave_tables(sources):
    pieces = 3
    rows = sources * pieces
    waves = 2 * rows
    points = waves * LANES
    order = np.array([source * pieces + piece for piece in range(pieces) for source in range(sources)])
    wave = np.arange(rows + 1)
    lane = np.arange(LANES)

    first = np.zeros((2 * HALF, rows))
    angle = 2.0 * np.pi * (wave[:, None] * order[None, :] % waves) / waves
    first[: rows + 1] = np.cos(angle)
    first[HALF : HALF + rows + 1] = -np.sin(angle)

    weight = np.where((wave == 0) | (wave == rows), 1.0, 2.0) / points
    last = np.zeros((rows, 2 * HALF))
    last[:, : rows + 1] = np.cos(angle).T * weight
    last[:, HALF : HALF + rows + 1] = -np.sin(angle).T * weight

    twist = np.zeros((2, HALF, LANES))
    turn = 2.0 * np.pi * (wave[:, None] * lane[None, :] % points) / points
    twist[0, : rows + 1] = np.cos(turn)
    twist[1, : rows + 1] = np.sin(turn)

    spin = 2.0 * np.pi * (lane[:, None] * lane[None, :] % LANES) / LANES
    cos, sin = np.cos(spin), np.sin(spin)
    middle = np.block([[cos, -sin], [sin, cos]])
    back = np.block([[cos, sin], [-sin, cos]])

    first_high, first_low = split_table(first)
    last_high, last_low = split_table(last)
    return (
        np.concatenate([first_high, first_low], axis=1),
        np.concatenate([first_high, first_low, first_high], axis=1),
        np.concatenate([last_high, last_low], axis=1),
        middle.astype(ml_dtypes.bfloat16),
        back.astype(ml_dtypes.bfloat16),
        twist.astype(np.float32),
    )


def dot(left, right):
    return jnp.dot(left, right, preferred_element_type=F32)


def take_rows(wide, group, sources, channels):
    columns = []
    for c in range(GROUP):
        start = group * GROUP + c
        columns.append(
            jnp.concatenate(
                [wide[j, pl.ds(start, sources, stride=channels), :] for j in range(3)], axis=0
            )
        )
    return jnp.concatenate(columns, axis=1)


def put_rows(wide, group, sources, channels, rows):
    for c in range(GROUP):
        start = group * GROUP + c
        for j in range(3):
            wide[j, pl.ds(start, sources, stride=channels), :] = rows[
                j * sources : (j + 1) * sources, c * LANES : (c + 1) * LANES
            ]


def forward(stacked, first, twist, middle):
    cos, sin = twist[0], twist[1]
    waves = dot(first, stacked)
    rows = []
    for c in range(GROUP):
        real = waves[:HALF, c * LANES : (c + 1) * LANES]
        imag = waves[HALF:, c * LANES : (c + 1) * LANES]
        rows.append(
            jnp.concatenate([real * cos + imag * sin, imag * cos - real * sin], axis=1)
        )
    return dot(jnp.concatenate(rows, axis=0).astype(BF16), middle)


def inverse(real, imag, back, twist, last):
    cos, sin = twist[0], twist[1]
    turned = dot(jnp.concatenate([real, imag], axis=1).astype(BF16), back)
    columns = []
    for c in range(GROUP):
        zr = turned[c * HALF : (c + 1) * HALF, :LANES]
        zi = turned[c * HALF : (c + 1) * HALF, LANES:]
        columns.append(
            jnp.concatenate([zr * cos - zi * sin, zr * sin + zi * cos], axis=0)
        )
    waves = jnp.concatenate(columns, axis=1).astype(BF16)
    return dot(last, jnp.concatenate([waves, waves], axis=0))


def kernel(
    scale,
    sources,
    channels,
    query_hbm,
    key_hbm,
    value_hbm,
    cotan_hbm,
    taps_hbm,
    first_hbm,
    first_wide_hbm,
    last_hbm,
    middle_hbm,
    back_hbm,
    twist_hbm,
    out_hbm,
    gquery_hbm,
    gkey_hbm,
    gvalue_hbm,
    gfilter_hbm,
    query,
    key,
    value,
    cotan,
    taps,
    first,
    first_wide,
    last,
    middle,
    back,
    twist,
    out_buf,
    gfilter,
    gate_send,
    back_send,
    gate_recv,
    back_recv,
    conv_send,
    bconv_send,
    conv_recv,
    bconv_recv,
    wide_in,
    wide_out,
    filt_spec,
    gate_spec,
    core_send,
    core_recv,
    x_send,
    x_recv,
    z_send,
    z_recv,
    total,
    load_sem,
    store_sem,
    send_sem,
    recv_sem,
    red_send,
    red_recv,
):
    me = lax.axis_index("ctx")
    rep = lax.axis_index("rep")
    zl = rep // 8
    xc = rep // 2 % 4
    core = rep % 2
    tokens = 3 * LANES
    groups = channels // GROUP

    barrier = pltpu.get_barrier_semaphore()

    def greet(step, carry):
        peer = lax.rem(me + step, sources)
        pl.semaphore_signal(barrier, inc=1, device_id=(rep, peer), device_id_type=MESH)
        return carry

    other_core = rep + 1 - 2 * core
    other_z = (1 - zl) * 8 + xc * 2 + core

    def x_peer(step):
        return zl * 8 + lax.rem(xc + step, 4) * 2 + core

    lax.fori_loop(1, sources, greet, 0)
    for peer in [other_core, other_z] + [x_peer(step) for step in range(1, 4)]:
        pl.semaphore_signal(barrier, inc=1, device_id=(peer, me), device_id_type=MESH)

    loads = []
    for index, (src, dst) in enumerate(
        [
            (key_hbm, key),
            (value_hbm, value),
            (cotan_hbm, cotan),
            (query_hbm, query),
            (taps_hbm, taps),
            (first_hbm, first),
            (first_wide_hbm, first_wide),
            (last_hbm, last),
            (middle_hbm, middle),
            (back_hbm, back),
            (twist_hbm, twist),
        ]
    ):
        load = pltpu.make_async_copy(src, dst, load_sem.at[index])
        load.start()
        loads.append(load)

    def products(left, right, held):
        def body(c, carry):
            lane = pl.ds(pl.multiple_of(c * LANES, LANES), LANES)
            for i in range(3):
                spot = pl.ds(i * LANES, LANES)
                both = left[spot, lane].astype(F32) * right[spot, lane].astype(F32)
                held[lane, spot] = both.T.astype(BF16)
            return carry

        lax.fori_loop(0, left.shape[1] // LANES, body, 0)

    def exchange(kind, held, landing):
        def copy(peer, sender):
            return pltpu.make_async_remote_copy(
                src_ref=held.at[pl.ds(peer * channels, channels), :],
                dst_ref=landing.at[sender],
                send_sem=send_sem.at[kind, peer],
                recv_sem=recv_sem.at[kind, sender],
                device_id=(rep, peer),
                device_id_type=MESH,
            )

        def start(step, carry):
            copy(lax.rem(me + step, sources), me).start()
            return carry

        def arrive(step, carry):
            peer = lax.rem(me + step, sources)
            copy(peer, peer).wait_recv()
            return carry

        def leave(step, carry):
            copy(lax.rem(me + step, sources), me).wait_send()
            return carry

        def go():
            lax.fori_loop(1, sources, start, 0)
            landing[me] = held[pl.ds(pl.multiple_of(me * channels, channels), channels), :]

        return (
            go,
            lambda: lax.fori_loop(1, sources, arrive, 0),
            lambda: lax.fori_loop(1, sources, leave, 0),
        )

    gate_go, gate_arrive, gate_leave = exchange(0, gate_send, gate_recv)
    back_go, back_arrive, back_leave = exchange(1, back_send, back_recv)
    conv_go, conv_arrive, conv_leave = exchange(2, conv_send, conv_recv)
    bconv_go, bconv_arrive, bconv_leave = exchange(3, bconv_send, bconv_recv)

    loads[0].wait()
    loads[1].wait()
    products(key, value, gate_send)
    loads[2].wait()
    loads[3].wait()
    products(cotan, query, back_send)

    pl.semaphore_wait(barrier, sources - 1 + 5)
    gate_go()
    back_go()

    loads[4].wait()
    for load in loads[5:]:
        load.wait()

    def turn_taps(s, carry):
        for j in range(3):
            spot = pl.ds(pl.multiple_of((s * 3 + j) * LANES, LANES), LANES)
            wide_in[j, pl.ds(pl.multiple_of(s * channels, channels), channels), :] = taps[spot, :].T
        return carry

    lax.fori_loop(0, sources, turn_taps, 0)

    def filter_group(g, carry):
        rows = take_rows(wide_in, g, sources, channels)
        high = rows.astype(BF16)
        low = (rows - high.astype(F32)).astype(BF16)
        filt_spec[g] = forward(
            jnp.concatenate([high, high, low], axis=0), first_wide[...], twist, middle[...]
        )
        return carry

    lax.fori_loop(0, groups, filter_group, 0)

    def widen(landing):
        def body(s, carry):
            for j in range(3):
                wide_in[j, pl.ds(pl.multiple_of(s * channels, channels), channels), :] = landing[
                    s, :, j * LANES : (j + 1) * LANES
                ].astype(F32)
            return carry

        lax.fori_loop(0, sources, body, 0)

    def narrow(held):
        def body(s, carry):
            spot = pl.ds(pl.multiple_of(s * channels, channels), channels)
            for j in range(3):
                held[spot, j * LANES : (j + 1) * LANES] = wide_out[j, spot, :].astype(BF16)
            return carry

        lax.fori_loop(0, sources, body, 0)

    def spectrum(g):
        rows = take_rows(wide_in, g, sources, channels).astype(BF16)
        return forward(jnp.concatenate([rows, rows], axis=0), first[...], twist, middle[...])

    gate_arrive()
    widen(gate_recv)

    def conv_group(g, carry):
        spec = spectrum(g)
        gate_spec[g] = spec
        gr, gi = spec[:, :LANES], spec[:, LANES:]
        hr, hi = filt_spec[g, :, :LANES], filt_spec[g, :, LANES:]
        rows = inverse(gr * hr - gi * hi, gr * hi + gi * hr, back[...], twist, last[...])
        put_rows(wide_out, g, sources, channels, rows)
        return carry

    lax.fori_loop(0, groups, conv_group, 0)
    narrow(conv_send)
    conv_go()

    back_arrive()
    widen(back_recv)

    def bconv_group(g, carry):
        spec = spectrum(g)
        br, bi = spec[:, :LANES], spec[:, LANES:]
        hr, hi = filt_spec[g, :, :LANES], filt_spec[g, :, LANES:]
        rows = inverse(br * hr + bi * hi, bi * hr - br * hi, back[...], twist, last[...])
        put_rows(wide_out, g, sources, channels, rows)
        gr, gi = gate_spec[g, :, :LANES], gate_spec[g, :, LANES:]
        gate_spec[g] = jnp.concatenate([br * gr + bi * gi, bi * gr - br * gi], axis=1)
        return carry

    lax.fori_loop(0, groups, bconv_group, 0)
    narrow(bconv_send)
    bconv_go()

    def term_group(g, carry):
        rows = inverse(
            gate_spec[g, :, :LANES], gate_spec[g, :, LANES:], back[...], twist, last[...]
        )
        put_rows(wide_out, g, sources, channels, rows)
        return carry

    lax.fori_loop(0, groups, term_group, 0)

    def term_rows(where):
        spot = pl.ds(pl.multiple_of(where * channels, channels), channels)
        return [wide_out[j, spot, :] for j in range(3)]

    def fill_core(i, carry):
        where = i % 2 * 8 + i // 2 * 2 + 1 - core
        for j, rows in enumerate(term_rows(where)):
            core_send[i, :, j * LANES : (j + 1) * LANES] = rows.astype(BF16)
        return carry

    lax.fori_loop(0, 8, fill_core, 0)
    core_copy = pltpu.make_async_remote_copy(
        src_ref=core_send,
        dst_ref=core_recv,
        send_sem=red_send.at[0],
        recv_sem=red_recv.at[0],
        device_id=(other_core, me),
        device_id_type=MESH,
    )
    core_copy.start()

    def results(landing, parts):
        def body(c, carry):
            lane = pl.ds(pl.multiple_of(c * LANES, LANES), LANES)
            for i in range(3):
                spot = pl.ds(i * LANES, LANES)
                block = landing[pl.ds(c * 4, 4), :, i * LANES : (i + 1) * LANES]
                rows = block.reshape(LANES, LANES).astype(F32).T
                for other, held in parts:
                    held[spot, lane] = (other[spot, lane].astype(F32) * rows).astype(BF16)
            return carry

        lax.fori_loop(0, query.shape[1] // LANES, body, 0)

    def store(index, src, dst):
        copy = pltpu.make_async_copy(src, dst, store_sem.at[index])
        copy.start()
        return copy

    conv_arrive()
    results(conv_recv, [(query, out_buf.at[0]), (cotan, out_buf.at[1])])
    stores = [store(0, out_buf.at[0], out_hbm), store(1, out_buf.at[1], gquery_hbm)]

    core_copy.wait()

    def add_core(i, carry):
        where = i % 2 * 8 + i // 2 * 2 + core
        for j, rows in enumerate(term_rows(where)):
            lane = slice(j * LANES, (j + 1) * LANES)
            added = rows + core_recv[i, :, lane].astype(F32)
            total[i, :, lane] = added
            x_send[i, :, lane] = added.astype(BF16)
        return carry

    lax.fori_loop(0, 8, add_core, 0)
    x_copies = []
    for step in range(1, 4):
        there = lax.rem(xc + step, 4)
        copy = pltpu.make_async_remote_copy(
            src_ref=x_send.at[pl.ds(there * 2, 2)],
            dst_ref=x_recv.at[step - 1],
            send_sem=red_send.at[step],
            recv_sem=red_recv.at[step],
            device_id=(x_peer(step), me),
            device_id_type=MESH,
        )
        copy.start()
        x_copies.append(copy)
    for copy in x_copies:
        copy.wait()

    def x_sum(which):
        added = total[xc * 2 + which]
        for step in range(3):
            added = added + x_recv[step, which].astype(F32)
        return added

    z_send[...] = x_sum(1 - zl).astype(BF16)
    z_copy = pltpu.make_async_remote_copy(
        src_ref=z_send,
        dst_ref=z_recv,
        send_sem=red_send.at[4],
        recv_sem=red_recv.at[4],
        device_id=(other_z, me),
        device_id_type=MESH,
    )
    z_copy.start()
    own = x_sum(zl)
    z_copy.wait()
    summed = (own + z_recv[...].astype(F32)) * scale
    for j in range(3):
        gfilter[j * LANES : (j + 1) * LANES, :] = summed[:, j * LANES : (j + 1) * LANES].T
    stores.append(store(4, gfilter, gfilter_hbm))

    bconv_arrive()
    results(bconv_recv, [(value, out_buf.at[2]), (key, out_buf.at[3])])
    stores += [store(2, out_buf.at[2], gkey_hbm), store(3, out_buf.at[3], gvalue_hbm)]
    gate_leave()
    back_leave()
    conv_leave()
    bconv_leave()
    for copy in stores:
        copy.wait()


def on_device(tables, query_feat, key_feat, value_feat, filter_taps, out_cotangent):
    tokens, width = query_feat.shape[1:]
    sources = lax.axis_size("ctx")
    channels = width // sources
    groups = channels // GROUP
    scale = 1.0 / math.sqrt(lax.axis_size("rep") * tokens * sources)
    seq = jax.ShapeDtypeStruct((tokens, width), BF16)
    anywhere = pl.BlockSpec(memory_space=pl.ANY)
    block = (sources, channels, tokens)
    vmem = pltpu.VMEM
    outs = pl.pallas_call(
        functools.partial(kernel, scale, sources, channels),
        out_shape=(seq, seq, seq, seq, jax.ShapeDtypeStruct((tokens, channels), F32)),
        in_specs=[anywhere] * (5 + len(tables)),
        out_specs=(anywhere,) * 5,
        scratch_shapes=[
            vmem((tokens, width), BF16),
            vmem((tokens, width), BF16),
            vmem((tokens, width), BF16),
            vmem((tokens, width), BF16),
            vmem(filter_taps.shape, F32),
            *[vmem(table.shape, table.dtype) for table in tables],
            vmem((4, tokens, width), BF16),
            vmem((tokens, channels), F32),
            vmem((width, tokens), BF16),
            vmem((width, tokens), BF16),
            vmem(block, BF16),
            vmem(block, BF16),
            vmem((width, tokens), BF16),
            vmem((width, tokens), BF16),
            vmem(block, BF16),
            vmem(block, BF16),
            vmem((3, sources * channels, LANES), F32),
            vmem((3, sources * channels, LANES), F32),
            vmem((groups, GROUP * HALF, 2 * LANES), F32),
            vmem((groups, GROUP * HALF, 2 * LANES), F32),
            vmem((8, channels, tokens), BF16),
            vmem((8, channels, tokens), BF16),
            vmem((8, channels, tokens), BF16),
            vmem((3, 2, channels, tokens), BF16),
            vmem((channels, tokens), BF16),
            vmem((channels, tokens), BF16),
            vmem((8, channels, tokens), F32),
            pltpu.SemaphoreType.DMA((5 + len(tables),)),
            pltpu.SemaphoreType.DMA((5,)),
            pltpu.SemaphoreType.DMA((4, sources)),
            pltpu.SemaphoreType.DMA((4, sources)),
            pltpu.SemaphoreType.DMA((5,)),
            pltpu.SemaphoreType.DMA((5,)),
        ],
        compiler_params=pltpu.CompilerParams(
            collective_id=0, has_side_effects=True, vmem_limit_bytes=48 * 2**20
        ),
    )(
        query_feat[0],
        key_feat[0],
        value_feat[0],
        out_cotangent[0],
        filter_taps,
        *[jnp.asarray(table) for table in tables],
    )
    return (*[out[None] for out in outs[:4]], outs[4])


def solution(mesh):
    tables = wave_tables(mesh.shape["ctx"])
    rows = P("rep", "ctx", None)
    return jax.shard_map(
        functools.partial(on_device, tables),
        mesh=mesh,
        in_specs=(rows, rows, rows, P(None, "ctx"), rows),
        out_specs=(rows, rows, rows, rows, P("rep", "ctx")),
        check_vma=False,
    )
```

```python
import functools
import math

import jax
import jax.numpy as jnp
import ml_dtypes
import numpy as np
from jax import lax
from jax.experimental import pallas as pl
from jax.experimental.pallas import tpu as pltpu
from jax.sharding import PartitionSpec as P

MESH = pl.DeviceIdType.MESH
F32 = jnp.float32
BF16 = jnp.bfloat16
LANES = 128
HALF = 56
GROUP = 4


def split_table(table):
    high = table.astype(ml_dtypes.bfloat16)
    low = (table - high.astype(np.float64)).astype(ml_dtypes.bfloat16)
    return high, low


def wave_tables(sources):
    pieces = 3
    rows = sources * pieces
    waves = 2 * rows
    points = waves * LANES
    order = np.array([source * pieces + piece for piece in range(pieces) for source in range(sources)])
    wave = np.arange(rows + 1)
    lane = np.arange(LANES)

    first = np.zeros((2 * HALF, rows))
    angle = 2.0 * np.pi * (wave[:, None] * order[None, :] % waves) / waves
    first[: rows + 1] = np.cos(angle)
    first[HALF : HALF + rows + 1] = -np.sin(angle)

    weight = np.where((wave == 0) | (wave == rows), 1.0, 2.0) / points
    last = np.zeros((rows, 2 * HALF))
    last[:, : rows + 1] = np.cos(angle).T * weight
    last[:, HALF : HALF + rows + 1] = -np.sin(angle).T * weight

    twist = np.zeros((2, HALF, LANES))
    turn = 2.0 * np.pi * (wave[:, None] * lane[None, :] % points) / points
    twist[0, : rows + 1] = np.cos(turn)
    twist[1, : rows + 1] = np.sin(turn)

    spin = 2.0 * np.pi * (lane[:, None] * lane[None, :] % LANES) / LANES
    cos, sin = np.cos(spin), np.sin(spin)
    middle = np.block([[cos, -sin], [sin, cos]])
    back = np.block([[cos, sin], [-sin, cos]])

    first_high, first_low = split_table(first)
    last_high, last_low = split_table(last)
    parts = (
        np.concatenate([first_high, first_low, first_high], axis=1),
        np.concatenate([last_high, last_low], axis=1),
        middle,
        back,
        np.concatenate([twist[0], twist[1]], axis=1),
    )
    width = 2 * LANES
    return np.concatenate(
        [np.pad(part.astype(np.float32), ((0, 0), (0, width - part.shape[1]))) for part in parts]
    )


def dot(left, right):
    return jnp.dot(left, right, preferred_element_type=F32)


def take_rows(wide, group, sources, channels):
    columns = []
    for c in range(GROUP):
        start = group * GROUP + c
        columns.append(
            jnp.concatenate(
                [wide[j, pl.ds(start, sources, stride=channels), :] for j in range(3)], axis=0
            )
        )
    return jnp.concatenate(columns, axis=1)


def put_rows(wide, group, sources, channels, rows):
    for c in range(GROUP):
        start = group * GROUP + c
        for j in range(3):
            wide[j, pl.ds(start, sources, stride=channels), :] = rows[
                j * sources : (j + 1) * sources, c * LANES : (c + 1) * LANES
            ]


def forward(stacked, first, twist, middle):
    cos, sin = twist[0], twist[1]
    waves = dot(first, stacked)
    rows = []
    for c in range(GROUP):
        real = waves[:HALF, c * LANES : (c + 1) * LANES]
        imag = waves[HALF:, c * LANES : (c + 1) * LANES]
        rows.append(
            jnp.concatenate([real * cos + imag * sin, imag * cos - real * sin], axis=1)
        )
    return dot(jnp.concatenate(rows, axis=0).astype(BF16), middle)


def inverse(real, imag, back, twist, last):
    cos, sin = twist[0], twist[1]
    turned = dot(jnp.concatenate([real, imag], axis=1).astype(BF16), back)
    columns = []
    for c in range(GROUP):
        zr = turned[c * HALF : (c + 1) * HALF, :LANES]
        zi = turned[c * HALF : (c + 1) * HALF, LANES:]
        columns.append(
            jnp.concatenate([zr * cos - zi * sin, zr * sin + zi * cos], axis=0)
        )
    waves = jnp.concatenate(columns, axis=1).astype(BF16)
    return dot(last, jnp.concatenate([waves, waves], axis=0))


def kernel(
    scale,
    sources,
    channels,
    query_hbm,
    key_hbm,
    value_hbm,
    cotan_hbm,
    taps_hbm,
    tables_hbm,
    conv_recv,
    bconv_recv,
    gfilter,
    query,
    key,
    value,
    cotan,
    taps,
    tables,
    first,
    last,
    middle,
    back,
    twist,
    gate_send,
    back_send,
    gate_recv,
    back_recv,
    conv_send,
    bconv_send,
    wide_in,
    wide_out,
    filt_spec,
    gate_spec,
    core_send,
    core_recv,
    x_send,
    x_recv,
    z_send,
    z_recv,
    total,
    load_sem,
    own_sem,
    send_sem,
    recv_sem,
    red_send,
    red_recv,
):
    me = lax.axis_index("ctx")
    rep = lax.axis_index("rep")
    zl = rep // 8
    xc = rep // 2 % 4
    core = rep % 2
    tokens = 3 * LANES
    groups = channels // GROUP

    barrier = pltpu.get_barrier_semaphore()

    def greet(step, carry):
        peer = lax.rem(me + step, sources)
        pl.semaphore_signal(barrier, inc=1, device_id=(rep, peer), device_id_type=MESH)
        return carry

    other_core = rep + 1 - 2 * core
    other_z = (1 - zl) * 8 + xc * 2 + core

    def x_peer(step):
        return zl * 8 + lax.rem(xc + step, 4) * 2 + core

    lax.fori_loop(1, sources, greet, 0)
    for peer in [other_core, other_z] + [x_peer(step) for step in range(1, 4)]:
        pl.semaphore_signal(barrier, inc=1, device_id=(peer, me), device_id_type=MESH)

    loads = []
    for index, (src, dst) in enumerate(
        [
            (key_hbm, key),
            (value_hbm, value),
            (cotan_hbm, cotan),
            (query_hbm, query),
            (taps_hbm, taps),
            (tables_hbm, tables),
        ]
    ):
        load = pltpu.make_async_copy(src, dst, load_sem.at[index])
        load.start()
        loads.append(load)

    def products(left, right, held):
        def body(c, carry):
            lane = pl.ds(pl.multiple_of(c * LANES, LANES), LANES)
            for i in range(3):
                spot = pl.ds(i * LANES, LANES)
                both = left[spot, lane].astype(F32) * right[spot, lane].astype(F32)
                held[lane, spot] = both.T.astype(BF16)
            return carry

        lax.fori_loop(0, left.shape[1] // LANES, body, 0)

    def own(kind, held, landing):
        return pltpu.make_async_copy(
            held.at[pl.ds(pl.multiple_of(me * channels, channels), channels), :],
            landing.at[me],
            own_sem.at[kind],
        )

    def exchange(kind, held, landing):
        def copy(peer, sender):
            return pltpu.make_async_remote_copy(
                src_ref=held.at[pl.ds(peer * channels, channels), :],
                dst_ref=landing.at[sender],
                send_sem=send_sem.at[kind, peer],
                recv_sem=recv_sem.at[kind, sender],
                device_id=(rep, peer),
                device_id_type=MESH,
            )

        def start(step, carry):
            copy(lax.rem(me + step, sources), me).start()
            return carry

        def arrive(step, carry):
            peer = lax.rem(me + step, sources)
            copy(peer, peer).wait_recv()
            return carry

        def leave(step, carry):
            copy(lax.rem(me + step, sources), me).wait_send()
            return carry

        def go():
            lax.fori_loop(1, sources, start, 0)
            own(kind, held, landing).start()

        def arrive_all():
            own(kind, held, landing).wait()
            lax.fori_loop(1, sources, arrive, 0)

        return (
            go,
            arrive_all,
            lambda: lax.fori_loop(1, sources, leave, 0),
        )

    gate_go, gate_arrive, gate_leave = exchange(0, gate_send, gate_recv)
    back_go, back_arrive, back_leave = exchange(1, back_send, back_recv)
    conv_go, conv_arrive, conv_leave = exchange(2, conv_send, conv_recv)
    bconv_go, bconv_arrive, bconv_leave = exchange(3, bconv_send, bconv_recv)

    loads[0].wait()
    loads[1].wait()
    products(key, value, gate_send)
    with jax.named_scope("barrier"):
        pl.semaphore_wait(barrier, sources - 1 + 5)
    with jax.named_scope("gate_go"):
        gate_go()
    loads[2].wait()
    loads[3].wait()
    with jax.named_scope("back_products"):
        products(cotan, query, back_send)
    with jax.named_scope("back_go"):
        back_go()

    loads[4].wait()
    loads[5].wait()
    rows = 0
    for held in (first, last, middle, back):
        held[...] = tables[rows : rows + held.shape[0], : held.shape[1]].astype(BF16)
        rows += held.shape[0]
    for part in range(2):
        twist[part] = tables[rows : rows + HALF, part * LANES : (part + 1) * LANES]

    def turn_taps(s, carry):
        for j in range(3):
            spot = pl.ds(pl.multiple_of((s * 3 + j) * LANES, LANES), LANES)
            wide_in[j, pl.ds(pl.multiple_of(s * channels, channels), channels), :] = taps[:, spot]
        return carry

    lax.fori_loop(0, sources, turn_taps, 0)

    def filter_group(g, carry):
        rows = take_rows(wide_in, g, sources, channels)
        high = rows.astype(BF16)
        low = (rows - high.astype(F32)).astype(BF16)
        filt_spec[g] = forward(
            jnp.concatenate([high, high, low], axis=0), first[...], twist, middle[...]
        )
        return carry

    lax.fori_loop(0, groups, filter_group, 0)

    def widen(landing):
        def body(s, carry):
            for j in range(3):
                wide_in[j, pl.ds(pl.multiple_of(s * channels, channels), channels), :] = landing[
                    s, :, j * LANES : (j + 1) * LANES
                ].astype(F32)
            return carry

        lax.fori_loop(0, sources, body, 0)

    def narrow(held):
        def body(s, carry):
            spot = pl.ds(pl.multiple_of(s * channels, channels), channels)
            for j in range(3):
                held[spot, j * LANES : (j + 1) * LANES] = wide_out[j, spot, :].astype(BF16)
            return carry

        lax.fori_loop(0, sources, body, 0)

    def spectrum(g):
        rows = take_rows(wide_in, g, sources, channels).astype(BF16)
        return forward(jnp.concatenate([rows, rows], axis=0), first[:, : 2 * sources * 3], twist, middle[...])

    gate_arrive()
    widen(gate_recv)

    def conv_group(g, carry):
        spec = spectrum(g)
        gate_spec[g] = spec
        gr, gi = spec[:, :LANES], spec[:, LANES:]
        hr, hi = filt_spec[g, :, :LANES], filt_spec[g, :, LANES:]
        rows = inverse(gr * hr - gi * hi, gr * hi + gi * hr, back[...], twist, last[...])
        put_rows(wide_out, g, sources, channels, rows)
        return carry

    lax.fori_loop(0, groups, conv_group, 0)
    narrow(conv_send)
    conv_go()

    back_arrive()
    widen(back_recv)

    def bconv_group(g, carry):
        spec = spectrum(g)
        br, bi = spec[:, :LANES], spec[:, LANES:]
        hr, hi = filt_spec[g, :, :LANES], filt_spec[g, :, LANES:]
        rows = inverse(br * hr + bi * hi, bi * hr - br * hi, back[...], twist, last[...])
        put_rows(wide_out, g, sources, channels, rows)
        gr, gi = gate_spec[g, :, :LANES], gate_spec[g, :, LANES:]
        gate_spec[g] = jnp.concatenate([br * gr + bi * gi, bi * gr - br * gi], axis=1)
        return carry

    lax.fori_loop(0, groups, bconv_group, 0)
    narrow(bconv_send)
    bconv_go()

    def term_group(g, carry):
        rows = inverse(
            gate_spec[g, :, :LANES], gate_spec[g, :, LANES:], back[...], twist, last[...]
        )
        put_rows(wide_out, g, sources, channels, rows)
        return carry

    lax.fori_loop(0, groups, term_group, 0)

    def term_rows(where):
        spot = pl.ds(pl.multiple_of(where * channels, channels), channels)
        return [wide_out[j, spot, :] for j in range(3)]

    def fill_core(i, carry):
        where = i % 2 * 8 + i // 2 * 2 + 1 - core
        for j, rows in enumerate(term_rows(where)):
            core_send[i, :, j * LANES : (j + 1) * LANES] = rows.astype(BF16)
        return carry

    lax.fori_loop(0, 8, fill_core, 0)
    core_copy = pltpu.make_async_remote_copy(
        src_ref=core_send,
        dst_ref=core_recv,
        send_sem=red_send.at[0],
        recv_sem=red_recv.at[0],
        device_id=(other_core, me),
        device_id_type=MESH,
    )
    core_copy.start()

    core_copy.wait()

    def add_core(i, carry):
        where = i % 2 * 8 + i // 2 * 2 + core
        for j, rows in enumerate(term_rows(where)):
            lane = slice(j * LANES, (j + 1) * LANES)
            added = rows + core_recv[i, :, lane].astype(F32)
            total[i, :, lane] = added
            x_send[i, :, lane] = added.astype(BF16)
        return carry

    lax.fori_loop(0, 8, add_core, 0)
    x_copies = []
    for step in range(1, 4):
        there = lax.rem(xc + step, 4)
        copy = pltpu.make_async_remote_copy(
            src_ref=x_send.at[pl.ds(there * 2, 2)],
            dst_ref=x_recv.at[step - 1],
            send_sem=red_send.at[step],
            recv_sem=red_recv.at[step],
            device_id=(x_peer(step), me),
            device_id_type=MESH,
        )
        copy.start()
        x_copies.append(copy)
    for copy in x_copies:
        copy.wait()

    def x_sum(which):
        added = total[xc * 2 + which]
        for step in range(3):
            added = added + x_recv[step, which].astype(F32)
        return added

    z_send[...] = x_sum(1 - zl).astype(BF16)
    z_copy = pltpu.make_async_remote_copy(
        src_ref=z_send,
        dst_ref=z_recv,
        send_sem=red_send.at[4],
        recv_sem=red_recv.at[4],
        device_id=(other_z, me),
        device_id_type=MESH,
    )
    z_copy.start()
    mine = x_sum(zl)
    z_copy.wait()
    summed = (mine + z_recv[...].astype(F32)) * scale
    gfilter[...] = summed

    conv_arrive()
    bconv_arrive()
    gate_leave()
    back_leave()
    conv_leave()
    bconv_leave()


def finish(
    conv_hbm,
    bconv_hbm,
    term_hbm,
    query_hbm,
    key_hbm,
    value_hbm,
    cotan_hbm,
    out_hbm,
    gquery_hbm,
    gkey_hbm,
    gvalue_hbm,
    gfilter_hbm,
    conv,
    bconv,
    term,
    query,
    key,
    value,
    cotan,
    out_buf,
    load_sem,
    store_sem,
):
    loads = []
    for index, (src, dst) in enumerate(
        [
            (bconv_hbm, bconv),
            (key_hbm, key),
            (value_hbm, value),
            (conv_hbm, conv),
            (query_hbm, query),
            (cotan_hbm, cotan),
            (term_hbm, term),
        ]
    ):
        load = pltpu.make_async_copy(src, dst, load_sem.at[index])
        load.start()
        loads.append(load)
    stores = []

    def results(landing, parts):
        for c in range(query.shape[1] // LANES):
            lane = slice(c * LANES, (c + 1) * LANES)
            for i in range(3):
                spot = slice(i * LANES, (i + 1) * LANES)
                rows = landing[lane, spot].astype(F32).T
                for which, other, dst in parts:
                    out_buf[which, spot, lane] = (other[spot, lane].astype(F32) * rows).astype(BF16)
            for which, other, dst in parts:
                copy = pltpu.make_async_copy(
                    out_buf.at[which, :, lane], dst.at[:, lane], store_sem.at[which, c]
                )
                copy.start()
                stores.append(copy)

    for load in loads[:3]:
        load.wait()
    results(bconv, [(2, value, gkey_hbm), (3, key, gvalue_hbm)])
    for load in loads[3:]:
        load.wait()
    copy = pltpu.make_async_copy(term, gfilter_hbm, load_sem.at[0])
    copy.start()
    stores.append(copy)
    results(conv, [(0, query, out_hbm), (1, cotan, gquery_hbm)])
    for copy in stores:
        copy.wait()


def on_device(tables, query_feat, key_feat, value_feat, filter_taps, out_cotangent):
    tokens, width = query_feat.shape[1:]
    sources = lax.axis_size("ctx")
    channels = width // sources
    groups = channels // GROUP
    rows = sources * 3
    scale = 1.0 / math.sqrt(lax.axis_size("rep") * tokens * sources)
    anywhere = pl.BlockSpec(memory_space=pl.ANY)
    block = (sources, channels, tokens)
    landing = jax.ShapeDtypeStruct(block, BF16)
    vmem = pltpu.VMEM
    features = (query_feat[0], key_feat[0], value_feat[0], out_cotangent[0])
    conv, bconv, term = pl.pallas_call(
        functools.partial(kernel, scale, sources, channels),
        out_shape=(landing, landing, jax.ShapeDtypeStruct((channels, tokens), F32)),
        in_specs=[pl.BlockSpec(memory_space=pltpu.HBM)] * 6,
        out_specs=(anywhere, anywhere, pl.BlockSpec(memory_space=pltpu.VMEM)),
        scratch_shapes=[
            *[vmem((tokens, width), BF16)] * 4,
            vmem(filter_taps.shape[::-1], F32),
            vmem(tables.shape, F32),
            vmem((2 * HALF, 3 * rows), BF16),
            vmem((rows, 4 * HALF), BF16),
            vmem((2 * LANES, 2 * LANES), BF16),
            vmem((2 * LANES, 2 * LANES), BF16),
            vmem((2, HALF, LANES), F32),
            vmem((width, tokens), BF16),
            vmem((width, tokens), BF16),
            vmem(block, BF16),
            vmem(block, BF16),
            vmem((width, tokens), BF16),
            vmem((width, tokens), BF16),
            vmem((3, sources * channels, LANES), F32),
            vmem((3, sources * channels, LANES), F32),
            vmem((groups, GROUP * HALF, 2 * LANES), F32),
            vmem((groups, GROUP * HALF, 2 * LANES), F32),
            vmem((8, channels, tokens), BF16),
            vmem((8, channels, tokens), BF16),
            vmem((8, channels, tokens), BF16),
            vmem((3, 2, channels, tokens), BF16),
            vmem((channels, tokens), BF16),
            vmem((channels, tokens), BF16),
            vmem((8, channels, tokens), F32),
            pltpu.SemaphoreType.DMA((6,)),
            pltpu.SemaphoreType.DMA((4,)),
            pltpu.SemaphoreType.DMA((4, sources)),
            pltpu.SemaphoreType.DMA((4, sources)),
            pltpu.SemaphoreType.DMA((5,)),
            pltpu.SemaphoreType.DMA((5,)),
        ],
        compiler_params=pltpu.CompilerParams(
            collective_id=0, has_side_effects=True, vmem_limit_bytes=60 * 2**20
        ),
    )(*features, filter_taps.T, jnp.asarray(tables))
    seq = jax.ShapeDtypeStruct((tokens, width), BF16)
    outs = pl.pallas_call(
        finish,
        out_shape=(seq, seq, seq, seq, jax.ShapeDtypeStruct((channels, tokens), F32)),
        in_specs=[anywhere] * 7,
        out_specs=(anywhere,) * 5,
        scratch_shapes=[
            vmem((width, tokens), BF16),
            vmem((width, tokens), BF16),
            vmem((channels, tokens), F32),
            *[vmem((tokens, width), BF16)] * 4,
            vmem((4, tokens, width), BF16),
            pltpu.SemaphoreType.DMA((7,)),
            pltpu.SemaphoreType.DMA((4, width // LANES)),
        ],
        compiler_params=pltpu.CompilerParams(vmem_limit_bytes=60 * 2**20),
    )(conv.reshape(width, tokens), bconv.reshape(width, tokens), term, *features)
    return (*[out[None] for out in outs[:4]], outs[4].T)


def solution(mesh):
    tables = wave_tables(mesh.shape["ctx"])
    rows = P("rep", "ctx", None)
    return jax.shard_map(
        functools.partial(on_device, tables),
        mesh=mesh,
        in_specs=(rows, rows, rows, P(None, "ctx"), rows),
        out_specs=(rows, rows, rows, rows, P("rep", "ctx")),
        check_vma=False,
    )
```

```python
import functools
import math

import jax
import jax.numpy as jnp
import ml_dtypes
import numpy as np
from jax import lax
from jax.experimental import pallas as pl
from jax.experimental.pallas import tpu as pltpu
from jax.sharding import PartitionSpec as P

MESH = pl.DeviceIdType.MESH
F32 = jnp.float32
BF16 = jnp.bfloat16
LANES = 128
HALF = 56
GROUP = 16


def split_table(table):
    high = table.astype(ml_dtypes.bfloat16)
    low = (table - high.astype(np.float64)).astype(ml_dtypes.bfloat16)
    return high, low


def wave_tables(sources):
    pieces = 3
    rows = sources * pieces
    waves = 2 * rows
    points = waves * LANES
    order = np.array([source * pieces + piece for piece in range(pieces) for source in range(sources)])
    wave = np.arange(rows + 1)
    lane = np.arange(LANES)

    first = np.zeros((2 * HALF, rows))
    angle = 2.0 * np.pi * (wave[:, None] * order[None, :] % waves) / waves
    first[: rows + 1] = np.cos(angle)
    first[HALF : HALF + rows + 1] = -np.sin(angle)

    weight = np.where((wave == 0) | (wave == rows), 1.0, 2.0) / points
    last = np.zeros((rows, 2 * HALF))
    last[:, : rows + 1] = np.cos(angle).T * weight
    last[:, HALF : HALF + rows + 1] = -np.sin(angle).T * weight

    twist = np.zeros((2, HALF, LANES))
    turn = 2.0 * np.pi * (wave[:, None] * lane[None, :] % points) / points
    twist[0, : rows + 1] = np.cos(turn)
    twist[1, : rows + 1] = np.sin(turn)

    spin = 2.0 * np.pi * (lane[:, None] * lane[None, :] % LANES) / LANES
    cos, sin = np.cos(spin), np.sin(spin)
    middle = np.block([[cos, -sin], [sin, cos]])
    back = np.block([[cos, sin], [-sin, cos]])

    first_high, first_low = split_table(first)
    last_high, last_low = split_table(last)
    parts = (
        np.concatenate([first_high, first_low, first_high], axis=1),
        np.concatenate([last_high, last_low], axis=1),
        middle,
        back,
        np.concatenate([twist[0], twist[1]], axis=1),
    )
    width = 2 * LANES
    return np.concatenate(
        [np.pad(part.astype(np.float32), ((0, 0), (0, width - part.shape[1]))) for part in parts]
    )


def dot(left, right):
    return jnp.dot(left, right, preferred_element_type=F32)


def take_rows(wide, group, sources, channels):
    columns = []
    for c in range(GROUP):
        start = group * GROUP + c
        columns.append(
            jnp.concatenate(
                [wide[j, pl.ds(start, sources, stride=channels), :] for j in range(3)], axis=0
            )
        )
    return jnp.concatenate(columns, axis=1)


def put_rows(wide, group, sources, channels, rows):
    for c in range(GROUP):
        start = group * GROUP + c
        for j in range(3):
            wide[j, pl.ds(start, sources, stride=channels), :] = rows[
                j * sources : (j + 1) * sources, c * LANES : (c + 1) * LANES
            ]


def forward(stacked, first, twist, middle):
    cos, sin = twist[0], twist[1]
    waves = dot(first, stacked)
    rows = []
    for c in range(GROUP):
        real = waves[:HALF, c * LANES : (c + 1) * LANES]
        imag = waves[HALF:, c * LANES : (c + 1) * LANES]
        rows.append(
            jnp.concatenate([real * cos + imag * sin, imag * cos - real * sin], axis=1)
        )
    return dot(jnp.concatenate(rows, axis=0).astype(BF16), middle)


def inverse(real, imag, back, twist, last):
    cos, sin = twist[0], twist[1]
    turned = dot(jnp.concatenate([real, imag], axis=1).astype(BF16), back)
    columns = []
    for c in range(GROUP):
        zr = turned[c * HALF : (c + 1) * HALF, :LANES]
        zi = turned[c * HALF : (c + 1) * HALF, LANES:]
        columns.append(
            jnp.concatenate([zr * cos - zi * sin, zr * sin + zi * cos], axis=0)
        )
    waves = jnp.concatenate(columns, axis=1).astype(BF16)
    return dot(last, jnp.concatenate([waves, waves], axis=0))


def kernel(
    scale,
    sources,
    channels,
    query_hbm,
    key_hbm,
    value_hbm,
    cotan_hbm,
    taps_hbm,
    tables_hbm,
    out,
    gquery,
    gkey,
    gvalue,
    gfilter,
    query,
    key,
    value,
    cotan,
    taps,
    tables,
    first,
    last,
    middle,
    back,
    twist,
    gate_send,
    back_send,
    gate_recv,
    back_recv,
    conv_send,
    bconv_send,
    conv_recv,
    bconv_recv,
    wide_in,
    wide_out,
    filt_spec,
    gate_spec,
    core_send,
    core_recv,
    x_send,
    x_recv,
    z_send,
    z_recv,
    total,
    load_sem,
    own_sem,
    send_sem,
    recv_sem,
    last_sem,
    red_send,
    red_recv,
):
    me = lax.axis_index("ctx")
    rep = lax.axis_index("rep")
    rows_of = sources // 4
    z, y = me // rows_of, me % rows_of
    zl = rep // 8
    xc = rep // 2 % 4
    core = rep % 2
    tokens = 3 * LANES
    groups = channels // GROUP

    barrier = pltpu.get_barrier_semaphore()

    def greet(step, carry):
        peer = lax.rem(me + step, sources)
        pl.semaphore_signal(barrier, inc=1, device_id=(rep, peer), device_id_type=MESH)
        return carry

    other_core = rep + 1 - 2 * core
    other_z = (1 - zl) * 8 + xc * 2 + core

    def x_peer(step):
        return zl * 8 + lax.rem(xc + step, 4) * 2 + core

    lax.fori_loop(1, sources, greet, 0)
    for peer in [other_core, other_z] + [x_peer(step) for step in range(1, 4)]:
        pl.semaphore_signal(barrier, inc=1, device_id=(peer, me), device_id_type=MESH)

    loads = []
    for index, (src, dst) in enumerate(
        [
            (key_hbm, key),
            (value_hbm, value),
            (cotan_hbm, cotan),
            (query_hbm, query),
            (taps_hbm, taps),
            (tables_hbm, tables),
        ]
    ):
        load = pltpu.make_async_copy(src, dst, load_sem.at[index])
        load.start()
        loads.append(load)

    def products(left, right, held):
        def body(c, carry):
            lane = pl.ds(pl.multiple_of(c * LANES, LANES), LANES)
            for i in range(3):
                spot = pl.ds(i * LANES, LANES)
                both = left[spot, lane].astype(F32) * right[spot, lane].astype(F32)
                held[lane, spot] = both.T.astype(BF16)
            return carry

        lax.fori_loop(0, left.shape[1] // LANES, body, 0)

    far_first = (2, 1, 3, 0)

    def own(kind, held, landing):
        return pltpu.make_async_copy(
            held.at[pl.ds(pl.multiple_of(me * channels, channels), channels), :],
            landing.at[pl.ds(pl.multiple_of(me * channels, channels), channels), :],
            own_sem.at[kind],
        )

    def copies(kind, held, landing, count, peer, block, incoming):
        return pltpu.make_async_remote_copy(
            src_ref=held.at[pl.ds(block * channels, count * channels), :],
            dst_ref=landing.at[pl.ds(incoming * channels, count * channels), :],
            send_sem=send_sem.at[kind],
            recv_sem=recv_sem.at[kind],
            device_id=(rep, peer),
            device_id_type=MESH,
        )

    def exchange(kind, held, landing):
        def go():
            own(kind, held, landing).start()
            for dz in far_first:

                def start(step, carry):
                    peer = lax.rem(z + dz, 4) * rows_of + lax.rem(y + step, rows_of)
                    copies(kind, held, landing, 1, peer, peer, me).start()
                    return carry

                lax.fori_loop(0 if dz else 1, rows_of, start, 0)

        def whole():
            return copies(kind, held, landing, sources - 1, lax.rem(me + 1, sources), 0, 0)

        def arrive():
            own(kind, held, landing).wait()
            whole().wait_recv()

        return go, arrive, lambda: whole().wait_send()

    gate_go, gate_arrive, gate_leave = exchange(0, gate_send, gate_recv)
    back_go, back_arrive, back_leave = exchange(1, back_send, back_recv)
    conv_go, conv_arrive, conv_leave = exchange(2, conv_send, conv_recv)

    def last_copy(count, dz, peer, block, incoming):
        return pltpu.make_async_remote_copy(
            src_ref=bconv_send.at[pl.ds(block * channels, count * channels), :],
            dst_ref=bconv_recv.at[pl.ds(incoming * channels, count * channels), :],
            send_sem=send_sem.at[3],
            recv_sem=last_sem.at[dz],
            device_id=(rep, peer),
            device_id_type=MESH,
        )

    def bconv_go():
        own(3, bconv_send, bconv_recv).start()
        for dz in far_first:

            def start(step, carry):
                peer = lax.rem(z + dz, 4) * rows_of + lax.rem(y + step, rows_of)
                last_copy(1, dz, peer, peer, me).start()
                return carry

            lax.fori_loop(0 if dz else 1, rows_of, start, 0)

    def bconv_arrive(dz):
        if dz == 0:
            own(3, bconv_send, bconv_recv).wait()
        last_copy(rows_of - (dz == 0), dz, lax.rem(me + 1, sources), 0, 0).wait_recv()

    def bconv_leave():
        last_copy(sources - 1, 0, lax.rem(me + 1, sources), 0, 0).wait_send()

    loads[0].wait()
    loads[1].wait()
    products(key, value, gate_send)
    with jax.named_scope("barrier"):
        pl.semaphore_wait(barrier, sources - 1 + 5)
    with jax.named_scope("gate_go"):
        gate_go()
    loads[2].wait()
    loads[3].wait()
    with jax.named_scope("back_products"):
        products(cotan, query, back_send)
    with jax.named_scope("back_go"):
        back_go()

    loads[4].wait()
    loads[5].wait()
    rows = 0
    for held in (first, last, middle, back):
        held[...] = tables[rows : rows + held.shape[0], : held.shape[1]].astype(BF16)
        rows += held.shape[0]
    for part in range(2):
        twist[part] = tables[rows : rows + HALF, part * LANES : (part + 1) * LANES]

    def turn_taps(s, carry):
        for j in range(3):
            spot = pl.ds(pl.multiple_of((s * 3 + j) * LANES, LANES), LANES)
            wide_in[j, pl.ds(pl.multiple_of(s * channels, channels), channels), :] = taps[:, spot]
        return carry

    lax.fori_loop(0, sources, turn_taps, 0)

    def filter_group(g, carry):
        rows = take_rows(wide_in, g, sources, channels)
        high = rows.astype(BF16)
        low = (rows - high.astype(F32)).astype(BF16)
        filt_spec[g] = forward(
            jnp.concatenate([high, high, low], axis=0), first[...], twist, middle[...]
        )
        return carry

    lax.fori_loop(0, groups, filter_group, 0)

    def widen(landing):
        def body(s, carry):
            for j in range(3):
                spot = pl.ds(pl.multiple_of(s * channels, channels), channels)
                wide_in[j, spot, :] = landing[spot, j * LANES : (j + 1) * LANES].astype(F32)
            return carry

        lax.fori_loop(0, sources, body, 0)

    def narrow(held):
        def body(s, carry):
            spot = pl.ds(pl.multiple_of(s * channels, channels), channels)
            for j in range(3):
                held[spot, j * LANES : (j + 1) * LANES] = wide_out[j, spot, :].astype(BF16)
            return carry

        lax.fori_loop(0, sources, body, 0)

    def spectrum(g):
        rows = take_rows(wide_in, g, sources, channels).astype(BF16)
        return forward(jnp.concatenate([rows, rows], axis=0), first[:, : 2 * sources * 3], twist, middle[...])

    gate_arrive()
    widen(gate_recv)

    def conv_group(g, carry):
        spec = spectrum(g)
        gate_spec[g] = spec
        gr, gi = spec[:, :LANES], spec[:, LANES:]
        hr, hi = filt_spec[g, :, :LANES], filt_spec[g, :, LANES:]
        rows = inverse(gr * hr - gi * hi, gr * hi + gi * hr, back[...], twist, last[...])
        put_rows(wide_out, g, sources, channels, rows)
        return carry

    lax.fori_loop(0, groups, conv_group, 0)
    narrow(conv_send)
    conv_go()

    back_arrive()
    widen(back_recv)

    def bconv_group(g, carry):
        spec = spectrum(g)
        br, bi = spec[:, :LANES], spec[:, LANES:]
        hr, hi = filt_spec[g, :, :LANES], filt_spec[g, :, LANES:]
        rows = inverse(br * hr + bi * hi, bi * hr - br * hi, back[...], twist, last[...])
        put_rows(wide_out, g, sources, channels, rows)
        gr, gi = gate_spec[g, :, :LANES], gate_spec[g, :, LANES:]
        gate_spec[g] = jnp.concatenate([br * gr + bi * gi, bi * gr - br * gi], axis=1)
        return carry

    lax.fori_loop(0, groups, bconv_group, 0)
    narrow(bconv_send)
    bconv_go()

    def term_group(g, carry):
        rows = inverse(
            gate_spec[g, :, :LANES], gate_spec[g, :, LANES:], back[...], twist, last[...]
        )
        put_rows(wide_out, g, sources, channels, rows)
        return carry

    lax.fori_loop(0, groups, term_group, 0)

    def term_rows(where):
        spot = pl.ds(pl.multiple_of(where * channels, channels), channels)
        return [wide_out[j, spot, :] for j in range(3)]

    def fill_core(i, carry):
        where = i % 2 * 8 + i // 2 * 2 + 1 - core
        for j, rows in enumerate(term_rows(where)):
            core_send[i, :, j * LANES : (j + 1) * LANES] = rows.astype(BF16)
        return carry

    lax.fori_loop(0, 8, fill_core, 0)
    core_copy = pltpu.make_async_remote_copy(
        src_ref=core_send,
        dst_ref=core_recv,
        send_sem=red_send.at[0],
        recv_sem=red_recv.at[0],
        device_id=(other_core, me),
        device_id_type=MESH,
    )
    core_copy.start()

    core_copy.wait()

    def add_core(i, carry):
        where = i % 2 * 8 + i // 2 * 2 + core
        for j, rows in enumerate(term_rows(where)):
            lane = slice(j * LANES, (j + 1) * LANES)
            added = rows + core_recv[i, :, lane].astype(F32)
            total[i, :, lane] = added
            x_send[i, :, lane] = added.astype(BF16)
        return carry

    lax.fori_loop(0, 8, add_core, 0)
    x_copies = []
    for step in range(1, 4):
        there = lax.rem(xc + step, 4)
        copy = pltpu.make_async_remote_copy(
            src_ref=x_send.at[pl.ds(there * 2, 2)],
            dst_ref=x_recv.at[step - 1],
            send_sem=red_send.at[step],
            recv_sem=red_recv.at[step],
            device_id=(x_peer(step), me),
            device_id_type=MESH,
        )
        copy.start()
        x_copies.append(copy)
    for copy in x_copies:
        copy.wait()

    def x_sum(which):
        added = total[xc * 2 + which]
        for step in range(3):
            added = added + x_recv[step, which].astype(F32)
        return added

    z_send[...] = x_sum(1 - zl).astype(BF16)
    z_copy = pltpu.make_async_remote_copy(
        src_ref=z_send,
        dst_ref=z_recv,
        send_sem=red_send.at[4],
        recv_sem=red_recv.at[4],
        device_id=(other_z, me),
        device_id_type=MESH,
    )
    z_copy.start()
    mine = x_sum(zl)
    z_copy.wait()
    summed = (mine + z_recv[...].astype(F32)) * scale
    gfilter[...] = summed

    def results(which, landing, parts):
        lane = pl.ds(pl.multiple_of(which * LANES, LANES), LANES)
        for i in range(3):
            spot = pl.ds(i * LANES, LANES)
            rows = landing[lane, spot].astype(F32).T
            for other, held in parts:
                held[spot, lane] = (other[spot, lane].astype(F32) * rows).astype(BF16)

    gate_leave()
    back_leave()
    conv_arrive()

    def conv_results(which, carry):
        results(which, conv_recv, [(query, out), (cotan, gquery)])
        return carry

    lax.fori_loop(0, 4, conv_results, 0)
    conv_leave()
    for dz in far_first:
        bconv_arrive(dz)
        results(lax.rem(z + 4 - dz, 4), bconv_recv, [(value, gkey), (key, gvalue)])
    bconv_leave()


def store(*refs):
    held, results, sems = refs[:5], refs[5:10], refs[10]
    copies = [
        pltpu.make_async_copy(src, dst, sems.at[index])
        for index, (src, dst) in enumerate(zip(held, results))
    ]
    for copy in copies:
        copy.start()
    for copy in copies:
        copy.wait()


def on_device(tables, query_feat, key_feat, value_feat, filter_taps, out_cotangent):
    tokens, width = query_feat.shape[1:]
    sources = lax.axis_size("ctx")
    channels = width // sources
    groups = channels // GROUP
    rows = sources * 3
    scale = 1.0 / math.sqrt(lax.axis_size("rep") * tokens * sources)
    anywhere = pl.BlockSpec(memory_space=pl.ANY)
    inside = pl.BlockSpec(memory_space=pltpu.VMEM)
    vmem = pltpu.VMEM
    features = (query_feat[0], key_feat[0], value_feat[0], out_cotangent[0])
    held = pl.pallas_call(
        functools.partial(kernel, scale, sources, channels),
        out_shape=(*[vmem((tokens, width), BF16)] * 4, vmem((channels, tokens), F32)),
        in_specs=[pl.BlockSpec(memory_space=pltpu.HBM)] * 6,
        out_specs=(inside,) * 5,
        scratch_shapes=[
            *[vmem((tokens, width), BF16)] * 4,
            vmem(filter_taps.shape[::-1], F32),
            vmem(tables.shape, F32),
            vmem((2 * HALF, 3 * rows), BF16),
            vmem((rows, 4 * HALF), BF16),
            vmem((2 * LANES, 2 * LANES), BF16),
            vmem((2 * LANES, 2 * LANES), BF16),
            vmem((2, HALF, LANES), F32),
            vmem((width, tokens), BF16),
            vmem((width, tokens), BF16),
            vmem((width, tokens), BF16),
            vmem((width, tokens), BF16),
            vmem((width, tokens), BF16),
            vmem((width, tokens), BF16),
            vmem((width, tokens), BF16),
            vmem((width, tokens), BF16),
            vmem((3, sources * channels, LANES), F32),
            vmem((3, sources * channels, LANES), F32),
            vmem((groups, GROUP * HALF, 2 * LANES), F32),
            vmem((groups, GROUP * HALF, 2 * LANES), F32),
            vmem((8, channels, tokens), BF16),
            vmem((8, channels, tokens), BF16),
            vmem((8, channels, tokens), BF16),
            vmem((3, 2, channels, tokens), BF16),
            vmem((channels, tokens), BF16),
            vmem((channels, tokens), BF16),
            vmem((8, channels, tokens), F32),
            pltpu.SemaphoreType.DMA((6,)),
            pltpu.SemaphoreType.DMA((4,)),
            pltpu.SemaphoreType.DMA((4,)),
            pltpu.SemaphoreType.DMA((3,)),
            pltpu.SemaphoreType.DMA((4,)),
            pltpu.SemaphoreType.DMA((5,)),
            pltpu.SemaphoreType.DMA((5,)),
        ],
        compiler_params=pltpu.CompilerParams(
            collective_id=0, has_side_effects=True, vmem_limit_bytes=60 * 2**20
        ),
    )(*features, filter_taps.T, jnp.asarray(tables))
    seq = jax.ShapeDtypeStruct((tokens, width), BF16)
    outs = pl.pallas_call(
        store,
        out_shape=(seq, seq, seq, seq, jax.ShapeDtypeStruct((channels, tokens), F32)),
        in_specs=[inside] * 5,
        out_specs=(anywhere,) * 5,
        scratch_shapes=[pltpu.SemaphoreType.DMA((5,))],
        compiler_params=pltpu.CompilerParams(vmem_limit_bytes=4 * 2**20),
    )(*held)
    return (*[out[None] for out in outs[:4]], outs[4].T)


def solution(mesh):
    tables = wave_tables(mesh.shape["ctx"])
    rows = P("rep", "ctx", None)
    return jax.shard_map(
        functools.partial(on_device, tables),
        mesh=mesh,
        in_specs=(rows, rows, rows, P(None, "ctx"), rows),
        out_specs=(rows, rows, rows, rows, P("rep", "ctx")),
        check_vma=False,
    )
```

```python
import functools
import math

import jax
import jax.numpy as jnp
import ml_dtypes
import numpy as np
from jax import lax
from jax.experimental import pallas as pl
from jax.experimental.pallas import tpu as pltpu
from jax.sharding import PartitionSpec as P

MESH = pl.DeviceIdType.MESH
F32 = jnp.float32
BF16 = jnp.bfloat16
LANES = 128
HALF = 56
GROUP = 16


def split_table(table):
    high = table.astype(ml_dtypes.bfloat16)
    low = (table - high.astype(np.float64)).astype(ml_dtypes.bfloat16)
    return high, low


def wave_tables(sources):
    pieces = 3
    rows = sources * pieces
    waves = 2 * rows
    points = waves * LANES
    order = np.array([source * pieces + piece for piece in range(pieces) for source in range(sources)])
    wave = np.arange(rows + 1)
    lane = np.arange(LANES)

    first = np.zeros((2 * HALF, rows))
    angle = 2.0 * np.pi * (wave[:, None] * order[None, :] % waves) / waves
    first[: rows + 1] = np.cos(angle)
    first[HALF : HALF + rows + 1] = -np.sin(angle)

    weight = np.where((wave == 0) | (wave == rows), 1.0, 2.0) / points
    last = np.zeros((rows, 2 * HALF))
    last[:, : rows + 1] = np.cos(angle).T * weight
    last[:, HALF : HALF + rows + 1] = -np.sin(angle).T * weight

    twist = np.zeros((2, HALF, LANES))
    turn = 2.0 * np.pi * (wave[:, None] * lane[None, :] % points) / points
    twist[0, : rows + 1] = np.cos(turn)
    twist[1, : rows + 1] = np.sin(turn)

    spin = 2.0 * np.pi * (lane[:, None] * lane[None, :] % LANES) / LANES
    cos, sin = np.cos(spin), np.sin(spin)
    middle = np.block([[cos, -sin], [sin, cos]])
    back = np.block([[cos, sin], [-sin, cos]])

    first_high, first_low = split_table(first)
    last_high, last_low = split_table(last)
    parts = (
        np.concatenate([first_high, first_low, first_high], axis=1),
        np.concatenate([last_high, last_low], axis=1),
        middle,
        back,
        np.concatenate([twist[0], twist[1]], axis=1),
    )
    width = 2 * LANES
    return np.concatenate(
        [np.pad(part.astype(np.float32), ((0, 0), (0, width - part.shape[1]))) for part in parts]
    )


def dot(left, right):
    return jnp.dot(left, right, preferred_element_type=F32)


def take_rows(wide, group, sources, channels):
    columns = []
    for c in range(GROUP):
        start = group * GROUP + c
        columns.append(
            jnp.concatenate(
                [wide[j, pl.ds(start, sources, stride=channels), :] for j in range(3)], axis=0
            )
        )
    return jnp.concatenate(columns, axis=1)


def put_rows(wide, group, sources, channels, rows):
    for c in range(GROUP):
        start = group * GROUP + c
        for j in range(3):
            wide[j, pl.ds(start, sources, stride=channels), :] = rows[
                j * sources : (j + 1) * sources, c * LANES : (c + 1) * LANES
            ]


def forward(stacked, first, twist, middle):
    cos, sin = twist[0], twist[1]
    waves = dot(first, stacked)
    rows = []
    for c in range(GROUP):
        real = waves[:HALF, c * LANES : (c + 1) * LANES]
        imag = waves[HALF:, c * LANES : (c + 1) * LANES]
        rows.append(
            jnp.concatenate([real * cos + imag * sin, imag * cos - real * sin], axis=1)
        )
    return dot(jnp.concatenate(rows, axis=0).astype(BF16), middle)


def inverse(real, imag, back, twist, last):
    cos, sin = twist[0], twist[1]
    turned = dot(jnp.concatenate([real, imag], axis=1).astype(BF16), back)
    columns = []
    for c in range(GROUP):
        zr = turned[c * HALF : (c + 1) * HALF, :LANES]
        zi = turned[c * HALF : (c + 1) * HALF, LANES:]
        columns.append(
            jnp.concatenate([zr * cos - zi * sin, zr * sin + zi * cos], axis=0)
        )
    waves = jnp.concatenate(columns, axis=1).astype(BF16)
    return dot(last, jnp.concatenate([waves, waves], axis=0))


def kernel(
    scale,
    sources,
    channels,
    query_hbm,
    key_hbm,
    value_hbm,
    cotan_hbm,
    taps_hbm,
    tables_hbm,
    out,
    gquery,
    gkey,
    gvalue,
    gfilter,
    query,
    key,
    value,
    cotan,
    taps,
    tables,
    first,
    last,
    middle,
    back,
    twist,
    gate_send,
    back_send,
    gate_recv,
    back_recv,
    conv_send,
    bconv_send,
    conv_recv,
    bconv_recv,
    wide_in,
    wide_out,
    filt_spec,
    gate_spec,
    core_send,
    core_recv,
    x_send,
    x_recv,
    z_send,
    z_recv,
    total,
    load_sem,
    own_sem,
    send_sem,
    recv_sem,
    last_sem,
    red_send,
    red_recv,
    x_ready,
):
    me = lax.axis_index("ctx")
    rep = lax.axis_index("rep")
    rows_of = sources // 4
    z, y = me // rows_of, me % rows_of
    zl = rep // 8
    xc = rep // 2 % 4
    core = rep % 2
    tokens = 3 * LANES
    groups = channels // GROUP

    other_core = rep + 1 - 2 * core
    other_z = (1 - zl) * 8 + xc * 2 + core

    def x_peer(where):
        return zl * 8 + where * 2 + core

    barrier = pltpu.get_barrier_semaphore()

    def greet(peer, carry):
        pl.semaphore_signal(barrier, inc=1, device_id=(rep, peer), device_id_type=MESH)
        return carry

    def greet_x(where, carry):
        pl.semaphore_signal(barrier, inc=1, device_id=(x_peer(where), me), device_id_type=MESH)
        return carry

    lax.fori_loop(1, sources, lambda step, carry: greet(lax.rem(me + step, sources), carry), 0)
    lax.fori_loop(xc + 1, 4, greet_x, 0)
    for peer in (other_core, other_z):
        pl.semaphore_signal(barrier, inc=1, device_id=(peer, me), device_id_type=MESH)

    def report_x(where, carry):
        pl.semaphore_signal(
            x_ready.at[xc], inc=1, device_id=(x_peer(where), me), device_id_type=MESH
        )
        return carry

    loads = []
    for index, (src, dst) in enumerate(
        [
            (key_hbm, key),
            (value_hbm, value),
            (cotan_hbm, cotan),
            (query_hbm, query),
            (taps_hbm, taps),
            (tables_hbm, tables),
        ]
    ):
        load = pltpu.make_async_copy(src, dst, load_sem.at[index])
        load.start()
        loads.append(load)

    def products(left, right, held):
        def body(c, carry):
            lane = pl.ds(pl.multiple_of(c * LANES, LANES), LANES)
            for i in range(3):
                spot = pl.ds(i * LANES, LANES)
                both = left[spot, lane].astype(F32) * right[spot, lane].astype(F32)
                held[lane, spot] = both.T.astype(BF16)
            return carry

        lax.fori_loop(0, left.shape[1] // LANES, body, 0)

    far_first = (0, 1, 3, 2)

    def own(kind, held, landing):
        return pltpu.make_async_copy(
            held.at[pl.ds(pl.multiple_of(me * channels, channels), channels), :],
            landing.at[pl.ds(pl.multiple_of(me * channels, channels), channels), :],
            own_sem.at[kind],
        )

    def copies(kind, held, landing, count, peer, block, incoming):
        return pltpu.make_async_remote_copy(
            src_ref=held.at[pl.ds(block * channels, count * channels), :],
            dst_ref=landing.at[pl.ds(incoming * channels, count * channels), :],
            send_sem=send_sem.at[kind],
            recv_sem=recv_sem.at[kind],
            device_id=(rep, peer),
            device_id_type=MESH,
        )

    def exchange(kind, held, landing):
        def go():
            own(kind, held, landing).start()
            for dz in far_first:

                def start(step, carry):
                    peer = lax.rem(z + dz, 4) * rows_of + lax.rem(y + step, rows_of)
                    copies(kind, held, landing, 1, peer, peer, me).start()
                    return carry

                lax.fori_loop(0 if dz else 1, rows_of, start, 0)

        def whole():
            return copies(kind, held, landing, sources - 1, lax.rem(me + 1, sources), 0, 0)

        def arrive():
            own(kind, held, landing).wait()
            whole().wait_recv()

        return go, arrive, lambda: whole().wait_send()

    gate_go, gate_arrive, gate_leave = exchange(0, gate_send, gate_recv)
    back_go, back_arrive, back_leave = exchange(1, back_send, back_recv)
    conv_go, conv_arrive, conv_leave = exchange(2, conv_send, conv_recv)

    def last_copy(count, dz, peer, block, incoming):
        return pltpu.make_async_remote_copy(
            src_ref=bconv_send.at[pl.ds(block * channels, count * channels), :],
            dst_ref=bconv_recv.at[pl.ds(incoming * channels, count * channels), :],
            send_sem=send_sem.at[3],
            recv_sem=last_sem.at[dz],
            device_id=(rep, peer),
            device_id_type=MESH,
        )

    def bconv_go():
        own(3, bconv_send, bconv_recv).start()
        for dz in far_first:

            def start(step, carry):
                peer = lax.rem(z + dz, 4) * rows_of + lax.rem(y + step, rows_of)
                last_copy(1, dz, peer, peer, me).start()
                return carry

            lax.fori_loop(0 if dz else 1, rows_of, start, 0)

    def bconv_arrive(dz):
        if dz == 0:
            own(3, bconv_send, bconv_recv).wait()
        last_copy(rows_of - (dz == 0), dz, lax.rem(me + 1, sources), 0, 0).wait_recv()

    def bconv_leave():
        last_copy(sources - 1, 0, lax.rem(me + 1, sources), 0, 0).wait_send()

    loads[0].wait()
    loads[1].wait()
    products(key, value, gate_send)
    pl.semaphore_wait(barrier, sources + 1 + xc)
    gate_go()
    lax.fori_loop(0, xc, report_x, 0)
    loads[2].wait()
    loads[3].wait()
    products(cotan, query, back_send)
    back_go()

    loads[4].wait()
    loads[5].wait()
    rows = 0
    for held in (first, last, middle, back):
        held[...] = tables[rows : rows + held.shape[0], : held.shape[1]].astype(BF16)
        rows += held.shape[0]
    for part in range(2):
        twist[part] = tables[rows : rows + HALF, part * LANES : (part + 1) * LANES]

    def turn_taps(s, carry):
        for j in range(3):
            spot = pl.ds(pl.multiple_of((s * 3 + j) * LANES, LANES), LANES)
            wide_in[j, pl.ds(pl.multiple_of(s * channels, channels), channels), :] = taps[:, spot]
        return carry

    lax.fori_loop(0, sources, turn_taps, 0)

    def filter_group(g, carry):
        rows = take_rows(wide_in, g, sources, channels)
        high = rows.astype(BF16)
        low = (rows - high.astype(F32)).astype(BF16)
        filt_spec[g] = forward(
            jnp.concatenate([high, high, low], axis=0), first[...], twist, middle[...]
        )
        return carry

    lax.fori_loop(0, groups, filter_group, 0)

    def widen(landing):
        def body(s, carry):
            for j in range(3):
                spot = pl.ds(pl.multiple_of(s * channels, channels), channels)
                wide_in[j, spot, :] = landing[spot, j * LANES : (j + 1) * LANES].astype(F32)
            return carry

        lax.fori_loop(0, sources, body, 0)

    def narrow(held):
        def body(s, carry):
            spot = pl.ds(pl.multiple_of(s * channels, channels), channels)
            for j in range(3):
                held[spot, j * LANES : (j + 1) * LANES] = wide_out[j, spot, :].astype(BF16)
            return carry

        lax.fori_loop(0, sources, body, 0)

    def spectrum(g):
        rows = take_rows(wide_in, g, sources, channels).astype(BF16)
        return forward(jnp.concatenate([rows, rows], axis=0), first[:, : 2 * sources * 3], twist, middle[...])

    gate_arrive()
    widen(gate_recv)

    def conv_group(g, carry):
        spec = spectrum(g)
        gate_spec[g] = spec
        gr, gi = spec[:, :LANES], spec[:, LANES:]
        hr, hi = filt_spec[g, :, :LANES], filt_spec[g, :, LANES:]
        rows = inverse(gr * hr - gi * hi, gr * hi + gi * hr, back[...], twist, last[...])
        put_rows(wide_out, g, sources, channels, rows)
        return carry

    lax.fori_loop(0, groups, conv_group, 0)
    narrow(conv_send)
    conv_go()

    back_arrive()
    widen(back_recv)

    def bconv_group(g, carry):
        spec = spectrum(g)
        br, bi = spec[:, :LANES], spec[:, LANES:]
        hr, hi = filt_spec[g, :, :LANES], filt_spec[g, :, LANES:]
        rows = inverse(br * hr + bi * hi, bi * hr - br * hi, back[...], twist, last[...])
        put_rows(wide_out, g, sources, channels, rows)
        gr, gi = gate_spec[g, :, :LANES], gate_spec[g, :, LANES:]
        gate_spec[g] = jnp.concatenate([br * gr + bi * gi, bi * gr - br * gi], axis=1)
        return carry

    lax.fori_loop(0, groups, bconv_group, 0)
    narrow(bconv_send)
    bconv_go()

    def term_group(g, carry):
        rows = inverse(
            gate_spec[g, :, :LANES], gate_spec[g, :, LANES:], back[...], twist, last[...]
        )
        put_rows(wide_out, g, sources, channels, rows)
        return carry

    lax.fori_loop(0, groups, term_group, 0)

    def term_rows(where):
        spot = pl.ds(pl.multiple_of(where * channels, channels), channels)
        return [wide_out[j, spot, :] for j in range(3)]

    def fill_core(i, carry):
        where = i % 2 * 8 + i // 2 * 2 + 1 - core
        for j, rows in enumerate(term_rows(where)):
            core_send[i, :, j * LANES : (j + 1) * LANES] = rows.astype(BF16)
        return carry

    lax.fori_loop(0, 8, fill_core, 0)
    core_copy = pltpu.make_async_remote_copy(
        src_ref=core_send,
        dst_ref=core_recv,
        send_sem=red_send.at[0],
        recv_sem=red_recv.at[0],
        device_id=(other_core, me),
        device_id_type=MESH,
    )
    core_copy.start()

    core_copy.wait()

    def add_core(i, carry):
        where = i % 2 * 8 + i // 2 * 2 + core
        for j, rows in enumerate(term_rows(where)):
            lane = slice(j * LANES, (j + 1) * LANES)
            added = rows + core_recv[i, :, lane].astype(F32)
            total[i, :, lane] = added
            x_send[i, :, lane] = added.astype(BF16)
        return carry

    lax.fori_loop(0, 8, add_core, 0)

    def x_copy(where, sender, block):
        return pltpu.make_async_remote_copy(
            src_ref=x_send.at[pl.ds(block * 2, 2)],
            dst_ref=x_recv.at[sender],
            send_sem=red_send.at[1 + block],
            recv_sem=red_recv.at[1 + sender],
            device_id=(x_peer(where), me),
            device_id_type=MESH,
        )

    def x_start(where, carry):
        x_copy(where, xc, where).start()
        return carry

    def x_start_when_ready(where, carry):
        pl.semaphore_wait(x_ready.at[where], 1)
        return x_start(where, carry)

    def x_wait(step, carry):
        where = lax.rem(xc + step, 4)
        x_copy(where, where, where).wait()
        return carry

    lax.fori_loop(0, xc, x_start, 0)
    lax.fori_loop(xc + 1, 4, x_start_when_ready, 0)
    lax.fori_loop(1, 4, x_wait, 0)

    def x_sum(which):
        added = total[xc * 2 + which]
        for step in range(1, 4):
            added = added + x_recv[lax.rem(xc + step, 4), which].astype(F32)
        return added

    z_send[...] = x_sum(1 - zl).astype(BF16)
    z_copy = pltpu.make_async_remote_copy(
        src_ref=z_send,
        dst_ref=z_recv,
        send_sem=red_send.at[5],
        recv_sem=red_recv.at[5],
        device_id=(other_z, me),
        device_id_type=MESH,
    )
    z_copy.start()
    mine = x_sum(zl)
    z_copy.wait()
    summed = (mine + z_recv[...].astype(F32)) * scale
    gfilter[...] = summed

    def results(which, landing, parts):
        lane = pl.ds(pl.multiple_of(which * LANES, LANES), LANES)
        for i in range(3):
            spot = pl.ds(i * LANES, LANES)
            rows = landing[lane, spot].astype(F32).T
            for other, held in parts:
                held[spot, lane] = (other[spot, lane].astype(F32) * rows).astype(BF16)

    gate_leave()
    back_leave()
    conv_arrive()

    def conv_results(which, carry):
        results(which, conv_recv, [(query, out), (cotan, gquery)])
        return carry

    lax.fori_loop(0, 4, conv_results, 0)
    conv_leave()
    for dz in far_first:
        bconv_arrive(dz)
        results(lax.rem(z + 4 - dz, 4), bconv_recv, [(value, gkey), (key, gvalue)])
    bconv_leave()


def store(*refs):
    held, results, sems = refs[:5], refs[5:10], refs[10]
    copies = [
        pltpu.make_async_copy(src, dst, sems.at[index])
        for index, (src, dst) in enumerate(zip(held, results))
    ]
    for copy in copies:
        copy.start()
    for copy in copies:
        copy.wait()


def on_device(tables, query_feat, key_feat, value_feat, filter_taps, out_cotangent):
    tokens, width = query_feat.shape[1:]
    sources = lax.axis_size("ctx")
    channels = width // sources
    groups = channels // GROUP
    rows = sources * 3
    scale = 1.0 / math.sqrt(lax.axis_size("rep") * tokens * sources)
    anywhere = pl.BlockSpec(memory_space=pl.ANY)
    inside = pl.BlockSpec(memory_space=pltpu.VMEM)
    vmem = pltpu.VMEM
    features = (query_feat[0], key_feat[0], value_feat[0], out_cotangent[0])
    held = pl.pallas_call(
        functools.partial(kernel, scale, sources, channels),
        out_shape=(*[vmem((tokens, width), BF16)] * 4, vmem((channels, tokens), F32)),
        in_specs=[pl.BlockSpec(memory_space=pltpu.HBM)] * 6,
        out_specs=(inside,) * 5,
        scratch_shapes=[
            *[vmem((tokens, width), BF16)] * 4,
            vmem(filter_taps.shape[::-1], F32),
            vmem(tables.shape, F32),
            vmem((2 * HALF, 3 * rows), BF16),
            vmem((rows, 4 * HALF), BF16),
            vmem((2 * LANES, 2 * LANES), BF16),
            vmem((2 * LANES, 2 * LANES), BF16),
            vmem((2, HALF, LANES), F32),
            vmem((width, tokens), BF16),
            vmem((width, tokens), BF16),
            vmem((width, tokens), BF16),
            vmem((width, tokens), BF16),
            vmem((width, tokens), BF16),
            vmem((width, tokens), BF16),
            vmem((width, tokens), BF16),
            vmem((width, tokens), BF16),
            vmem((3, sources * channels, LANES), F32),
            vmem((3, sources * channels, LANES), F32),
            vmem((groups, GROUP * HALF, 2 * LANES), F32),
            vmem((groups, GROUP * HALF, 2 * LANES), F32),
            vmem((8, channels, tokens), BF16),
            vmem((8, channels, tokens), BF16),
            vmem((8, channels, tokens), BF16),
            vmem((4, 2, channels, tokens), BF16),
            vmem((channels, tokens), BF16),
            vmem((channels, tokens), BF16),
            vmem((8, channels, tokens), F32),
            pltpu.SemaphoreType.DMA((6,)),
            pltpu.SemaphoreType.DMA((4,)),
            pltpu.SemaphoreType.DMA((4,)),
            pltpu.SemaphoreType.DMA((3,)),
            pltpu.SemaphoreType.DMA((4,)),
            pltpu.SemaphoreType.DMA((6,)),
            pltpu.SemaphoreType.DMA((6,)),
            pltpu.SemaphoreType.REGULAR((4,)),
        ],
        compiler_params=pltpu.CompilerParams(
            collective_id=0, has_side_effects=True, vmem_limit_bytes=60 * 2**20
        ),
    )(*features, filter_taps.T, jnp.asarray(tables))
    seq = jax.ShapeDtypeStruct((tokens, width), BF16)
    outs = pl.pallas_call(
        store,
        out_shape=(seq, seq, seq, seq, jax.ShapeDtypeStruct((channels, tokens), F32)),
        in_specs=[inside] * 5,
        out_specs=(anywhere,) * 5,
        scratch_shapes=[pltpu.SemaphoreType.DMA((5,))],
        compiler_params=pltpu.CompilerParams(vmem_limit_bytes=4 * 2**20),
    )(*held)
    return (*[out[None] for out in outs[:4]], outs[4].T)


def solution(mesh):
    tables = wave_tables(mesh.shape["ctx"])
    rows = P("rep", "ctx", None)
    return jax.shard_map(
        functools.partial(on_device, tables),
        mesh=mesh,
        in_specs=(rows, rows, rows, P(None, "ctx"), rows),
        out_specs=(rows, rows, rows, rows, P("rep", "ctx")),
        check_vma=False,
    )
```

```python
import functools
import math

import jax
import jax.numpy as jnp
import ml_dtypes
import numpy as np
from jax import lax
from jax.experimental import pallas as pl
from jax.experimental.pallas import tpu as pltpu
from jax.sharding import PartitionSpec as P

MESH = pl.DeviceIdType.MESH
F32 = jnp.float32
BF16 = jnp.bfloat16
LANES = 128
HALF = 56
GROUP = 16


def split_table(table):
    high = table.astype(ml_dtypes.bfloat16)
    low = (table - high.astype(np.float64)).astype(ml_dtypes.bfloat16)
    return high, low


def wave_tables(sources):
    pieces = 3
    rows = sources * pieces
    waves = 2 * rows
    points = waves * LANES
    order = np.array([source * pieces + piece for piece in range(pieces) for source in range(sources)])
    wave = np.arange(rows + 1)
    lane = np.arange(LANES)

    first = np.zeros((2 * HALF, rows))
    angle = 2.0 * np.pi * (wave[:, None] * order[None, :] % waves) / waves
    first[: rows + 1] = np.cos(angle)
    first[HALF : HALF + rows + 1] = -np.sin(angle)

    weight = np.where((wave == 0) | (wave == rows), 1.0, 2.0) / points
    last = np.zeros((rows, 2 * HALF))
    last[:, : rows + 1] = np.cos(angle).T * weight
    last[:, HALF : HALF + rows + 1] = -np.sin(angle).T * weight

    twist = np.zeros((2, HALF, LANES))
    turn = 2.0 * np.pi * (wave[:, None] * lane[None, :] % points) / points
    twist[0, : rows + 1] = np.cos(turn)
    twist[1, : rows + 1] = np.sin(turn)

    spin = 2.0 * np.pi * (lane[:, None] * lane[None, :] % LANES) / LANES
    cos, sin = np.cos(spin), np.sin(spin)
    middle = np.block([[cos, -sin], [sin, cos]])
    back = np.block([[cos, sin], [-sin, cos]])

    first_high, first_low = split_table(first)
    middle_high, middle_low = split_table(middle)
    back_high, back_low = split_table(back)
    last_high, last_low = split_table(last)
    parts = (
        np.concatenate([first_high, first_low, first_high], axis=1),
        np.concatenate([last_high, last_low], axis=1),
        np.concatenate([middle_high, middle_low]),
        np.concatenate([back_high, back_low]),
        np.concatenate([twist[0], twist[1]], axis=1),
    )
    width = 2 * LANES
    return np.concatenate(
        [np.pad(part.astype(np.float32), ((0, 0), (0, width - part.shape[1]))) for part in parts]
    )


def dot(left, right):
    return jnp.dot(left, right, preferred_element_type=F32)


def two_parts(wide):
    high = wide.astype(BF16)
    return high, (wide - high.astype(F32)).astype(BF16)


def exact_dot(left, table):
    high, low = two_parts(left)
    return (
        dot(high, table[: 2 * LANES, :])
        + dot(low, table[: 2 * LANES, :])
        + dot(high, table[2 * LANES :, :])
    )


def rounded_dot(left, table):
    return dot(left.astype(BF16), table[: 2 * LANES, :])


def take_rows(wide, group, sources, channels):
    columns = []
    for c in range(GROUP):
        start = group * GROUP + c
        columns.append(
            jnp.concatenate(
                [wide[j, pl.ds(start, sources, stride=channels), :] for j in range(3)], axis=0
            )
        )
    return jnp.concatenate(columns, axis=1)


def put_rows(wide, group, sources, channels, rows):
    for c in range(GROUP):
        start = group * GROUP + c
        for j in range(3):
            wide[j, pl.ds(start, sources, stride=channels), :] = rows[
                j * sources : (j + 1) * sources, c * LANES : (c + 1) * LANES
            ]


def forward(stacked, first, twist, middle, multiply):
    cos, sin = twist[0], twist[1]
    waves = dot(first, stacked)
    rows = []
    for c in range(GROUP):
        real = waves[:HALF, c * LANES : (c + 1) * LANES]
        imag = waves[HALF:, c * LANES : (c + 1) * LANES]
        rows.append(
            jnp.concatenate([real * cos + imag * sin, imag * cos - real * sin], axis=1)
        )
    return multiply(jnp.concatenate(rows, axis=0), middle)


def inverse(real, imag, back, twist, last):
    cos, sin = twist[0], twist[1]
    turned = rounded_dot(jnp.concatenate([real, imag], axis=1), back)
    columns = []
    for c in range(GROUP):
        zr = turned[c * HALF : (c + 1) * HALF, :LANES]
        zi = turned[c * HALF : (c + 1) * HALF, LANES:]
        columns.append(
            jnp.concatenate([zr * cos - zi * sin, zr * sin + zi * cos], axis=0)
        )
    waves = jnp.concatenate(columns, axis=1).astype(BF16)
    return dot(last, jnp.concatenate([waves, waves], axis=0))


def kernel(
    scale,
    sources,
    channels,
    query_hbm,
    key_hbm,
    value_hbm,
    cotan_hbm,
    taps_hbm,
    tables_hbm,
    out,
    gquery,
    gkey,
    gvalue,
    gfilter,
    query,
    key,
    value,
    cotan,
    taps,
    tables,
    first,
    last,
    middle,
    back,
    twist,
    gate_send,
    back_send,
    gate_recv,
    back_recv,
    conv_send,
    bconv_send,
    conv_recv,
    bconv_recv,
    wide_in,
    wide_out,
    filt_spec,
    gate_spec,
    core_send,
    core_recv,
    x_send,
    x_recv,
    z_send,
    z_recv,
    total,
    load_sem,
    own_sem,
    send_sem,
    recv_sem,
    last_sem,
    red_send,
    red_recv,
    x_ready,
):
    me = lax.axis_index("ctx")
    rep = lax.axis_index("rep")
    rows_of = sources // 4
    z, y = me // rows_of, me % rows_of
    zl = rep // 8
    xc = rep // 2 % 4
    core = rep % 2
    groups = channels // GROUP

    other_core = rep + 1 - 2 * core
    other_z = (1 - zl) * 8 + xc * 2 + core

    def x_peer(where):
        return zl * 8 + where * 2 + core

    barrier = pltpu.get_barrier_semaphore()

    def greet(peer, carry):
        pl.semaphore_signal(barrier, inc=1, device_id=(rep, peer), device_id_type=MESH)
        return carry

    def greet_x(where, carry):
        pl.semaphore_signal(barrier, inc=1, device_id=(x_peer(where), me), device_id_type=MESH)
        return carry

    lax.fori_loop(1, sources, lambda step, carry: greet(lax.rem(me + step, sources), carry), 0)
    lax.fori_loop(xc + 1, 4, greet_x, 0)
    for peer in (other_core, other_z):
        pl.semaphore_signal(barrier, inc=1, device_id=(peer, me), device_id_type=MESH)

    def report_x(where, carry):
        pl.semaphore_signal(
            x_ready.at[xc], inc=1, device_id=(x_peer(where), me), device_id_type=MESH
        )
        return carry

    loads = []
    for index, (src, dst) in enumerate(
        [
            (key_hbm, key),
            (value_hbm, value),
            (cotan_hbm, cotan),
            (query_hbm, query),
            (taps_hbm, taps),
            (tables_hbm, tables),
        ]
    ):
        load = pltpu.make_async_copy(src, dst, load_sem.at[index])
        load.start()
        loads.append(load)

    def products(left, right, held):
        def body(c, carry):
            lane = pl.ds(pl.multiple_of(c * LANES, LANES), LANES)
            for i in range(3):
                spot = pl.ds(i * LANES, LANES)
                both = left[spot, lane].astype(F32) * right[spot, lane].astype(F32)
                held[lane, spot] = both.T.astype(BF16)
            return carry

        lax.fori_loop(0, left.shape[1] // LANES, body, 0)

    row_order = (0, 1, 3, 2)

    def own(kind, held, landing):
        return pltpu.make_async_copy(
            held.at[pl.ds(pl.multiple_of(me * channels, channels), channels), :],
            landing.at[pl.ds(pl.multiple_of(me * channels, channels), channels), :],
            own_sem.at[kind],
        )

    def copies(kind, held, landing, count, peer, block, incoming):
        return pltpu.make_async_remote_copy(
            src_ref=held.at[pl.ds(block * channels, count * channels), :],
            dst_ref=landing.at[pl.ds(incoming * channels, count * channels), :],
            send_sem=send_sem.at[kind],
            recv_sem=recv_sem.at[kind],
            device_id=(rep, peer),
            device_id_type=MESH,
        )

    def exchange(kind, held, landing):
        def go():
            own(kind, held, landing).start()
            for dz in row_order:

                def start(step, carry):
                    peer = lax.rem(z + dz, 4) * rows_of + lax.rem(y + step, rows_of)
                    copies(kind, held, landing, 1, peer, peer, me).start()
                    return carry

                lax.fori_loop(0 if dz else 1, rows_of, start, 0)

        def whole():
            return copies(kind, held, landing, sources - 1, lax.rem(me + 1, sources), 0, 0)

        def arrive():
            own(kind, held, landing).wait()
            whole().wait_recv()

        return go, arrive, lambda: whole().wait_send()

    gate_go, gate_arrive, gate_leave = exchange(0, gate_send, gate_recv)
    back_go, back_arrive, back_leave = exchange(1, back_send, back_recv)
    conv_go, conv_arrive, conv_leave = exchange(2, conv_send, conv_recv)

    def last_copy(count, dz, peer, block, incoming):
        return pltpu.make_async_remote_copy(
            src_ref=bconv_send.at[pl.ds(block * channels, count * channels), :],
            dst_ref=bconv_recv.at[pl.ds(incoming * channels, count * channels), :],
            send_sem=send_sem.at[3],
            recv_sem=last_sem.at[dz],
            device_id=(rep, peer),
            device_id_type=MESH,
        )

    def bconv_go():
        own(3, bconv_send, bconv_recv).start()
        for dz in row_order:

            def start(step, carry):
                peer = lax.rem(z + dz, 4) * rows_of + lax.rem(y + step, rows_of)
                last_copy(1, dz, peer, peer, me).start()
                return carry

            lax.fori_loop(0 if dz else 1, rows_of, start, 0)

    def bconv_arrive(dz):
        if dz == 0:
            own(3, bconv_send, bconv_recv).wait()
        last_copy(rows_of - (dz == 0), dz, lax.rem(me + 1, sources), 0, 0).wait_recv()

    def bconv_leave():
        last_copy(sources - 1, 0, lax.rem(me + 1, sources), 0, 0).wait_send()

    loads[0].wait()
    loads[1].wait()
    products(key, value, gate_send)
    pl.semaphore_wait(barrier, sources + 1 + xc)
    gate_go()
    lax.fori_loop(0, xc, report_x, 0)
    loads[2].wait()
    loads[3].wait()
    products(cotan, query, back_send)
    back_go()

    loads[4].wait()
    loads[5].wait()
    rows = 0
    for held in (first, last, middle, back):
        held[...] = tables[rows : rows + held.shape[0], : held.shape[1]].astype(BF16)
        rows += held.shape[0]
    for part in range(2):
        twist[part] = tables[rows : rows + HALF, part * LANES : (part + 1) * LANES]

    def turn_taps(s, carry):
        for j in range(3):
            spot = pl.ds(pl.multiple_of((s * 3 + j) * LANES, LANES), LANES)
            wide_in[j, pl.ds(pl.multiple_of(s * channels, channels), channels), :] = taps[:, spot]
        return carry

    lax.fori_loop(0, sources, turn_taps, 0)

    def filter_group(g, carry):
        rows = take_rows(wide_in, g, sources, channels)
        high, low = two_parts(rows)
        filt_spec[g] = forward(
            jnp.concatenate([high, high, low], axis=0), first[...], twist, middle, exact_dot
        )
        return carry

    lax.fori_loop(0, groups, filter_group, 0)

    def widen(landing):
        def body(s, carry):
            for j in range(3):
                spot = pl.ds(pl.multiple_of(s * channels, channels), channels)
                wide_in[j, spot, :] = landing[spot, j * LANES : (j + 1) * LANES].astype(F32)
            return carry

        lax.fori_loop(0, sources, body, 0)

    def narrow(held):
        def body(s, carry):
            spot = pl.ds(pl.multiple_of(s * channels, channels), channels)
            for j in range(3):
                held[spot, j * LANES : (j + 1) * LANES] = wide_out[j, spot, :].astype(BF16)
            return carry

        lax.fori_loop(0, sources, body, 0)

    def spectrum(g):
        rows = take_rows(wide_in, g, sources, channels).astype(BF16)
        return forward(jnp.concatenate([rows, rows], axis=0), first[:, : 2 * sources * 3], twist, middle, rounded_dot)

    gate_arrive()
    widen(gate_recv)

    def conv_group(g, carry):
        spec = spectrum(g)
        gate_spec[g] = spec
        gr, gi = spec[:, :LANES], spec[:, LANES:]
        hr, hi = filt_spec[g, :, :LANES], filt_spec[g, :, LANES:]
        rows = inverse(gr * hr - gi * hi, gr * hi + gi * hr, back, twist, last[...])
        put_rows(wide_out, g, sources, channels, rows)
        return carry

    lax.fori_loop(0, groups, conv_group, 0)
    narrow(conv_send)
    conv_go()

    back_arrive()
    widen(back_recv)

    def bconv_group(g, carry):
        spec = spectrum(g)
        br, bi = spec[:, :LANES], spec[:, LANES:]
        hr, hi = filt_spec[g, :, :LANES], filt_spec[g, :, LANES:]
        rows = inverse(br * hr + bi * hi, bi * hr - br * hi, back, twist, last[...])
        put_rows(wide_out, g, sources, channels, rows)
        gr, gi = gate_spec[g, :, :LANES], gate_spec[g, :, LANES:]
        gate_spec[g] = jnp.concatenate([br * gr + bi * gi, bi * gr - br * gi], axis=1)
        return carry

    lax.fori_loop(0, groups, bconv_group, 0)
    narrow(bconv_send)
    bconv_go()

    def term_group(g, carry):
        rows = inverse(
            gate_spec[g, :, :LANES], gate_spec[g, :, LANES:], back, twist, last[...]
        )
        put_rows(wide_out, g, sources, channels, rows)
        return carry

    lax.fori_loop(0, groups, term_group, 0)

    def term_rows(where):
        spot = pl.ds(pl.multiple_of(where * channels, channels), channels)
        return [wide_out[j, spot, :] for j in range(3)]

    def fill_core(i, carry):
        where = i % 2 * 8 + i // 2 * 2 + 1 - core
        for j, rows in enumerate(term_rows(where)):
            core_send[i, :, j * LANES : (j + 1) * LANES] = rows.astype(BF16)
        return carry

    lax.fori_loop(0, 8, fill_core, 0)
    core_copy = pltpu.make_async_remote_copy(
        src_ref=core_send,
        dst_ref=core_recv,
        send_sem=red_send.at[0],
        recv_sem=red_recv.at[0],
        device_id=(other_core, me),
        device_id_type=MESH,
    )
    core_copy.start()

    core_copy.wait()

    def add_core(i, carry):
        where = i % 2 * 8 + i // 2 * 2 + core
        for j, rows in enumerate(term_rows(where)):
            lane = slice(j * LANES, (j + 1) * LANES)
            added = rows + core_recv[i, :, lane].astype(F32)
            total[i, :, lane] = added
            x_send[i, :, lane] = added.astype(BF16)
        return carry

    lax.fori_loop(0, 8, add_core, 0)

    def x_copy(where, sender, block):
        return pltpu.make_async_remote_copy(
            src_ref=x_send.at[pl.ds(block * 2, 2)],
            dst_ref=x_recv.at[sender],
            send_sem=red_send.at[1 + block],
            recv_sem=red_recv.at[1 + sender],
            device_id=(x_peer(where), me),
            device_id_type=MESH,
        )

    def x_start(where, carry):
        x_copy(where, xc, where).start()
        return carry

    def x_start_when_ready(where, carry):
        pl.semaphore_wait(x_ready.at[where], 1)
        return x_start(where, carry)

    def x_wait(step, carry):
        where = lax.rem(xc + step, 4)
        x_copy(where, where, where).wait()
        return carry

    lax.fori_loop(0, xc, x_start, 0)
    lax.fori_loop(xc + 1, 4, x_start_when_ready, 0)
    lax.fori_loop(1, 4, x_wait, 0)

    def x_sum(which):
        added = total[xc * 2 + which]
        for step in range(1, 4):
            added = added + x_recv[lax.rem(xc + step, 4), which].astype(F32)
        return added

    z_send[...] = x_sum(1 - zl).astype(BF16)
    z_copy = pltpu.make_async_remote_copy(
        src_ref=z_send,
        dst_ref=z_recv,
        send_sem=red_send.at[5],
        recv_sem=red_recv.at[5],
        device_id=(other_z, me),
        device_id_type=MESH,
    )
    z_copy.start()
    mine = x_sum(zl)
    z_copy.wait()
    summed = (mine + z_recv[...].astype(F32)) * scale
    gfilter[...] = summed

    def results(which, landing, parts):
        lane = pl.ds(pl.multiple_of(which * LANES, LANES), LANES)
        for i in range(3):
            spot = pl.ds(i * LANES, LANES)
            rows = landing[lane, spot].astype(F32).T
            for other, held in parts:
                held[spot, lane] = (other[spot, lane].astype(F32) * rows).astype(BF16)

    gate_leave()
    back_leave()
    conv_arrive()

    def conv_results(which, carry):
        results(which, conv_recv, [(query, out), (cotan, gquery)])
        return carry

    lax.fori_loop(0, 4, conv_results, 0)
    conv_leave()
    for dz in row_order:
        bconv_arrive(dz)
        results(lax.rem(z + 4 - dz, 4), bconv_recv, [(value, gkey), (key, gvalue)])
    bconv_leave()


def store(*refs):
    held, results, sems = refs[:5], refs[5:10], refs[10]
    copies = [
        pltpu.make_async_copy(src, dst, sems.at[index])
        for index, (src, dst) in enumerate(zip(held, results))
    ]
    for copy in copies:
        copy.start()
    for copy in copies:
        copy.wait()


def on_device(tables, query_feat, key_feat, value_feat, filter_taps, out_cotangent):
    tokens, width = query_feat.shape[1:]
    sources = lax.axis_size("ctx")
    channels = width // sources
    groups = channels // GROUP
    rows = sources * 3
    scale = 1.0 / math.sqrt(lax.axis_size("rep") * tokens * sources)
    anywhere = pl.BlockSpec(memory_space=pl.ANY)
    inside = pl.BlockSpec(memory_space=pltpu.VMEM)
    vmem = pltpu.VMEM
    features = (query_feat[0], key_feat[0], value_feat[0], out_cotangent[0])
    held = pl.pallas_call(
        functools.partial(kernel, scale, sources, channels),
        out_shape=(*[vmem((tokens, width), BF16)] * 4, vmem((channels, tokens), F32)),
        in_specs=[pl.BlockSpec(memory_space=pltpu.HBM)] * 6,
        out_specs=(inside,) * 5,
        scratch_shapes=[
            *[vmem((tokens, width), BF16)] * 4,
            vmem(filter_taps.shape[::-1], F32),
            vmem(tables.shape, F32),
            vmem((2 * HALF, 3 * rows), BF16),
            vmem((rows, 4 * HALF), BF16),
            vmem((4 * LANES, 2 * LANES), BF16),
            vmem((4 * LANES, 2 * LANES), BF16),
            vmem((2, HALF, LANES), F32),
            vmem((width, tokens), BF16),
            vmem((width, tokens), BF16),
            vmem((width, tokens), BF16),
            vmem((width, tokens), BF16),
            vmem((width, tokens), BF16),
            vmem((width, tokens), BF16),
            vmem((width, tokens), BF16),
            vmem((width, tokens), BF16),
            vmem((3, sources * channels, LANES), F32),
            vmem((3, sources * channels, LANES), F32),
            vmem((groups, GROUP * HALF, 2 * LANES), F32),
            vmem((groups, GROUP * HALF, 2 * LANES), F32),
            vmem((8, channels, tokens), BF16),
            vmem((8, channels, tokens), BF16),
            vmem((8, channels, tokens), BF16),
            vmem((4, 2, channels, tokens), BF16),
            vmem((channels, tokens), BF16),
            vmem((channels, tokens), BF16),
            vmem((8, channels, tokens), F32),
            pltpu.SemaphoreType.DMA((6,)),
            pltpu.SemaphoreType.DMA((4,)),
            pltpu.SemaphoreType.DMA((4,)),
            pltpu.SemaphoreType.DMA((3,)),
            pltpu.SemaphoreType.DMA((4,)),
            pltpu.SemaphoreType.DMA((6,)),
            pltpu.SemaphoreType.DMA((6,)),
            pltpu.SemaphoreType.REGULAR((4,)),
        ],
        compiler_params=pltpu.CompilerParams(
            collective_id=0, has_side_effects=True, vmem_limit_bytes=60 * 2**20
        ),
    )(*features, filter_taps.T, jnp.asarray(tables))
    seq = jax.ShapeDtypeStruct((tokens, width), BF16)
    outs = pl.pallas_call(
        store,
        out_shape=(seq, seq, seq, seq, jax.ShapeDtypeStruct((channels, tokens), F32)),
        in_specs=[inside] * 5,
        out_specs=(anywhere,) * 5,
        scratch_shapes=[pltpu.SemaphoreType.DMA((5,))],
        compiler_params=pltpu.CompilerParams(vmem_limit_bytes=4 * 2**20),
    )(*held)
    return (*[out[None] for out in outs[:4]], outs[4].T)


def solution(mesh):
    tables = wave_tables(mesh.shape["ctx"])
    rows = P("rep", "ctx", None)
    return jax.shard_map(
        functools.partial(on_device, tables),
        mesh=mesh,
        in_specs=(rows, rows, rows, P(None, "ctx"), rows),
        out_specs=(rows, rows, rows, rows, P("rep", "ctx")),
        check_vma=False,
    )
```

```python
import functools
import math

import jax
import jax.numpy as jnp
import ml_dtypes
import numpy as np
from jax import lax
from jax.experimental import pallas as pl
from jax.experimental.pallas import tpu as pltpu
from jax.sharding import PartitionSpec as P

MESH = pl.DeviceIdType.MESH
F32 = jnp.float32
BF16 = jnp.bfloat16
LANES = 128
HALF = 56
GROUP = 16


def split_table(table):
    high = table.astype(ml_dtypes.bfloat16)
    low = (table - high.astype(np.float64)).astype(ml_dtypes.bfloat16)
    return high, low


def wave_tables(sources):
    pieces = 3
    rows = sources * pieces
    waves = 2 * rows
    points = waves * LANES
    order = np.array([source * pieces + piece for piece in range(pieces) for source in range(sources)])
    wave = np.arange(rows + 1)
    lane = np.arange(LANES)

    first = np.zeros((2 * HALF, rows))
    angle = 2.0 * np.pi * (wave[:, None] * order[None, :] % waves) / waves
    first[: rows + 1] = np.cos(angle)
    first[HALF : HALF + rows + 1] = -np.sin(angle)

    weight = np.where((wave == 0) | (wave == rows), 1.0, 2.0) / points
    last = np.zeros((rows, 2 * HALF))
    last[:, : rows + 1] = np.cos(angle).T * weight
    last[:, HALF : HALF + rows + 1] = -np.sin(angle).T * weight

    twist = np.zeros((2, HALF, LANES))
    turn = 2.0 * np.pi * (wave[:, None] * lane[None, :] % points) / points
    twist[0, : rows + 1] = np.cos(turn)
    twist[1, : rows + 1] = np.sin(turn)

    spin = 2.0 * np.pi * (lane[:, None] * lane[None, :] % LANES) / LANES
    cos, sin = np.cos(spin), np.sin(spin)
    middle = np.block([[cos, -sin], [sin, cos]])
    back = np.block([[cos, sin], [-sin, cos]])

    first_high, first_low = split_table(first)
    middle_high, middle_low = split_table(middle)
    back_high, back_low = split_table(back)
    last_high, last_low = split_table(last)
    parts = (
        np.concatenate([first_high, first_low, first_high], axis=1),
        np.concatenate([last_high, last_low], axis=1),
        np.concatenate([middle_high, middle_low]),
        np.concatenate([back_high, back_low]),
        np.concatenate([twist[0], twist[1]], axis=1),
    )
    width = 2 * LANES
    return np.concatenate(
        [np.pad(part.astype(np.float32), ((0, 0), (0, width - part.shape[1]))) for part in parts]
    )


def dot(left, right):
    return jnp.dot(left, right, preferred_element_type=F32)


def two_parts(wide):
    high = wide.astype(BF16)
    return high, (wide - high.astype(F32)).astype(BF16)


def exact_dot(left, table):
    high, low = two_parts(left)
    return (
        dot(high, table[: 2 * LANES, :])
        + dot(low, table[: 2 * LANES, :])
        + dot(high, table[2 * LANES :, :])
    )


def rounded_dot(left, table):
    return dot(left.astype(BF16), table[: 2 * LANES, :])


def take_rows(wide, group, sources, channels):
    columns = []
    for c in range(GROUP):
        start = group * GROUP + c
        columns.append(
            jnp.concatenate(
                [wide[j, pl.ds(start, sources, stride=channels), :] for j in range(3)], axis=0
            )
        )
    return jnp.concatenate(columns, axis=1)


def put_rows(wide, group, sources, channels, rows):
    for c in range(GROUP):
        start = group * GROUP + c
        for j in range(3):
            wide[j, pl.ds(start, sources, stride=channels), :] = rows[
                j * sources : (j + 1) * sources, c * LANES : (c + 1) * LANES
            ]


def forward(stacked, first, twist, middle, multiply):
    cos, sin = twist[0], twist[1]
    waves = dot(first, stacked)
    rows = []
    for c in range(GROUP):
        real = waves[:HALF, c * LANES : (c + 1) * LANES]
        imag = waves[HALF:, c * LANES : (c + 1) * LANES]
        rows.append(
            jnp.concatenate([real * cos + imag * sin, imag * cos - real * sin], axis=1)
        )
    return multiply(jnp.concatenate(rows, axis=0), middle)


def inverse(real, imag, back, twist, last):
    cos, sin = twist[0], twist[1]
    turned = rounded_dot(jnp.concatenate([real, imag], axis=1), back)
    columns = []
    for c in range(GROUP):
        zr = turned[c * HALF : (c + 1) * HALF, :LANES]
        zi = turned[c * HALF : (c + 1) * HALF, LANES:]
        columns.append(
            jnp.concatenate([zr * cos - zi * sin, zr * sin + zi * cos], axis=0)
        )
    waves = jnp.concatenate(columns, axis=1).astype(BF16)
    return dot(last, jnp.concatenate([waves, waves], axis=0))


def kernel(
    scale,
    sources,
    channels,
    query_hbm,
    key_hbm,
    value_hbm,
    cotan_hbm,
    taps_hbm,
    tables_hbm,
    out,
    gquery,
    gkey,
    gvalue,
    gfilter,
    query,
    key,
    value,
    cotan,
    taps,
    tables,
    first,
    last,
    middle,
    back,
    twist,
    gate_send,
    back_send,
    gate_recv,
    back_recv,
    conv_send,
    bconv_send,
    conv_recv,
    bconv_recv,
    wide_in,
    wide_out,
    filt_spec,
    gate_spec,
    core_send,
    core_recv,
    x_send,
    x_recv,
    z_send,
    z_recv,
    total,
    load_sem,
    own_sem,
    send_sem,
    recv_sem,
    last_sem,
    red_send,
    red_recv,
    x_ready,
):
    me = lax.axis_index("ctx")
    rep = lax.axis_index("rep")
    rows_of = sources // 4
    z, y = me // rows_of, me % rows_of
    zl = rep // 8
    xc = rep // 2 % 4
    core = rep % 2
    groups = channels // GROUP

    other_core = rep + 1 - 2 * core
    other_z = (1 - zl) * 8 + xc * 2 + core

    def x_peer(where):
        return zl * 8 + where * 2 + core

    barrier = pltpu.get_barrier_semaphore()

    def greet(peer, carry):
        pl.semaphore_signal(barrier, inc=1, device_id=(rep, peer), device_id_type=MESH)
        return carry

    def greet_x(where, carry):
        pl.semaphore_signal(barrier, inc=1, device_id=(x_peer(where), me), device_id_type=MESH)
        return carry

    lax.fori_loop(1, sources, lambda step, carry: greet(lax.rem(me + step, sources), carry), 0)
    lax.fori_loop(xc + 1, 4, greet_x, 0)
    for peer in (other_core, other_z):
        pl.semaphore_signal(barrier, inc=1, device_id=(peer, me), device_id_type=MESH)

    def report_x(where, carry):
        pl.semaphore_signal(
            x_ready.at[xc], inc=1, device_id=(x_peer(where), me), device_id_type=MESH
        )
        return carry

    loads = []
    for index, (src, dst) in enumerate(
        [
            (key_hbm, key),
            (value_hbm, value),
            (cotan_hbm, cotan),
            (query_hbm, query),
            (taps_hbm, taps),
            (tables_hbm, tables),
        ]
    ):
        load = pltpu.make_async_copy(src, dst, load_sem.at[index])
        load.start()
        loads.append(load)

    def products(left, right, held):
        def body(c, carry):
            lane = pl.ds(pl.multiple_of(c * LANES, LANES), LANES)
            for i in range(3):
                spot = pl.ds(i * LANES, LANES)
                both = left[spot, lane].astype(F32) * right[spot, lane].astype(F32)
                held[lane, spot] = both.T.astype(BF16)
            return carry

        lax.fori_loop(0, left.shape[1] // LANES, body, 0)

    row_order = (0, 1, 3, 2)

    def own(kind, held, landing):
        return pltpu.make_async_copy(
            held.at[pl.ds(pl.multiple_of(me * channels, channels), channels), :],
            landing.at[pl.ds(pl.multiple_of(me * channels, channels), channels), :],
            own_sem.at[kind],
        )

    def copies(kind, held, landing, count, peer, block, incoming):
        return pltpu.make_async_remote_copy(
            src_ref=held.at[pl.ds(block * channels, count * channels), :],
            dst_ref=landing.at[pl.ds(incoming * channels, count * channels), :],
            send_sem=send_sem.at[kind],
            recv_sem=recv_sem.at[kind],
            device_id=(rep, peer),
            device_id_type=MESH,
        )

    def exchange(kind, held, landing):
        def go():
            own(kind, held, landing).start()
            for turn in row_order:
                dz = lax.select(core == 0, turn, (4 - turn) % 4)

                def start(step, carry, dz=dz):
                    peer = lax.rem(z + dz, 4) * rows_of + lax.rem(y + step, rows_of)
                    copies(kind, held, landing, 1, peer, peer, me).start()
                    return carry

                lax.fori_loop(0 if turn else 1, rows_of, start, 0)

        def whole():
            return copies(kind, held, landing, sources - 1, lax.rem(me + 1, sources), 0, 0)

        def arrive():
            own(kind, held, landing).wait()
            whole().wait_recv()

        return go, arrive, lambda: whole().wait_send()

    gate_go, gate_arrive, gate_leave = exchange(0, gate_send, gate_recv)
    back_go, back_arrive, back_leave = exchange(1, back_send, back_recv)
    conv_go, conv_arrive, conv_leave = exchange(2, conv_send, conv_recv)

    def last_copy(count, dz, peer, block, incoming):
        return pltpu.make_async_remote_copy(
            src_ref=bconv_send.at[pl.ds(block * channels, count * channels), :],
            dst_ref=bconv_recv.at[pl.ds(incoming * channels, count * channels), :],
            send_sem=send_sem.at[3],
            recv_sem=last_sem.at[dz],
            device_id=(rep, peer),
            device_id_type=MESH,
        )

    def bconv_go():
        own(3, bconv_send, bconv_recv).start()
        for turn in row_order:
            dz = lax.select(core == 0, turn, (4 - turn) % 4)

            def start(step, carry, dz=dz):
                peer = lax.rem(z + dz, 4) * rows_of + lax.rem(y + step, rows_of)
                last_copy(1, dz, peer, peer, me).start()
                return carry

            lax.fori_loop(0 if turn else 1, rows_of, start, 0)

    def bconv_arrive(dz):
        if dz == 0:
            own(3, bconv_send, bconv_recv).wait()
        last_copy(rows_of - (dz == 0), dz, lax.rem(me + 1, sources), 0, 0).wait_recv()

    def bconv_leave():
        last_copy(sources - 1, 0, lax.rem(me + 1, sources), 0, 0).wait_send()

    loads[0].wait()
    loads[1].wait()
    products(key, value, gate_send)
    loads[2].wait()
    loads[3].wait()
    products(cotan, query, back_send)
    pl.semaphore_wait(barrier, sources + 1 + xc)
    gate_go()
    back_go()
    lax.fori_loop(0, xc, report_x, 0)

    loads[4].wait()
    loads[5].wait()
    rows = 0
    for held in (first, last, middle, back):
        held[...] = tables[rows : rows + held.shape[0], : held.shape[1]].astype(BF16)
        rows += held.shape[0]
    for part in range(2):
        twist[part] = tables[rows : rows + HALF, part * LANES : (part + 1) * LANES]

    def turn_taps(s, carry):
        for j in range(3):
            spot = pl.ds(pl.multiple_of((s * 3 + j) * LANES, LANES), LANES)
            wide_in[j, pl.ds(pl.multiple_of(s * channels, channels), channels), :] = taps[:, spot]
        return carry

    lax.fori_loop(0, sources, turn_taps, 0)

    def filter_group(g, carry):
        rows = take_rows(wide_in, g, sources, channels)
        high, low = two_parts(rows)
        filt_spec[g] = forward(
            jnp.concatenate([high, high, low], axis=0), first[...], twist, middle, exact_dot
        )
        return carry

    lax.fori_loop(0, groups, filter_group, 0)

    def widen(landing):
        def body(s, carry):
            for j in range(3):
                spot = pl.ds(pl.multiple_of(s * channels, channels), channels)
                wide_in[j, spot, :] = landing[spot, j * LANES : (j + 1) * LANES].astype(F32)
            return carry

        lax.fori_loop(0, sources, body, 0)

    def narrow(held):
        def body(s, carry):
            spot = pl.ds(pl.multiple_of(s * channels, channels), channels)
            for j in range(3):
                held[spot, j * LANES : (j + 1) * LANES] = wide_out[j, spot, :].astype(BF16)
            return carry

        lax.fori_loop(0, sources, body, 0)

    def spectrum(g):
        rows = take_rows(wide_in, g, sources, channels).astype(BF16)
        return forward(jnp.concatenate([rows, rows], axis=0), first[:, : 2 * sources * 3], twist, middle, rounded_dot)

    gate_arrive()
    widen(gate_recv)

    def conv_group(g, carry):
        spec = spectrum(g)
        gate_spec[g] = spec
        gr, gi = spec[:, :LANES], spec[:, LANES:]
        hr, hi = filt_spec[g, :, :LANES], filt_spec[g, :, LANES:]
        rows = inverse(gr * hr - gi * hi, gr * hi + gi * hr, back, twist, last[...])
        put_rows(wide_out, g, sources, channels, rows)
        return carry

    lax.fori_loop(0, groups, conv_group, 0)
    narrow(conv_send)
    conv_go()

    back_arrive()
    widen(back_recv)

    def bconv_group(g, carry):
        spec = spectrum(g)
        br, bi = spec[:, :LANES], spec[:, LANES:]
        hr, hi = filt_spec[g, :, :LANES], filt_spec[g, :, LANES:]
        rows = inverse(br * hr + bi * hi, bi * hr - br * hi, back, twist, last[...])
        put_rows(wide_out, g, sources, channels, rows)
        gr, gi = gate_spec[g, :, :LANES], gate_spec[g, :, LANES:]
        gate_spec[g] = jnp.concatenate([br * gr + bi * gi, bi * gr - br * gi], axis=1)
        return carry

    lax.fori_loop(0, groups, bconv_group, 0)
    narrow(bconv_send)
    bconv_go()

    def term_group(g, carry):
        rows = inverse(
            gate_spec[g, :, :LANES], gate_spec[g, :, LANES:], back, twist, last[...]
        )
        put_rows(wide_out, g, sources, channels, rows)
        return carry

    lax.fori_loop(0, groups, term_group, 0)

    def term_rows(where):
        spot = pl.ds(pl.multiple_of(where * channels, channels), channels)
        return [wide_out[j, spot, :] for j in range(3)]

    def fill_core(i, carry):
        where = i % 2 * 8 + i // 2 * 2 + 1 - core
        for j, rows in enumerate(term_rows(where)):
            core_send[i, :, j * LANES : (j + 1) * LANES] = rows.astype(BF16)
        return carry

    lax.fori_loop(0, 8, fill_core, 0)
    core_copy = pltpu.make_async_remote_copy(
        src_ref=core_send,
        dst_ref=core_recv,
        send_sem=red_send.at[0],
        recv_sem=red_recv.at[0],
        device_id=(other_core, me),
        device_id_type=MESH,
    )
    core_copy.start()

    core_copy.wait()

    def add_core(i, carry):
        where = i % 2 * 8 + i // 2 * 2 + core
        for j, rows in enumerate(term_rows(where)):
            lane = slice(j * LANES, (j + 1) * LANES)
            added = rows + core_recv[i, :, lane].astype(F32)
            total[i, :, lane] = added
            x_send[i, :, lane] = added.astype(BF16)
        return carry

    lax.fori_loop(0, 8, add_core, 0)

    def x_copy(where, sender, block):
        return pltpu.make_async_remote_copy(
            src_ref=x_send.at[pl.ds(block * 2, 2)],
            dst_ref=x_recv.at[sender],
            send_sem=red_send.at[1 + block],
            recv_sem=red_recv.at[1 + sender],
            device_id=(x_peer(where), me),
            device_id_type=MESH,
        )

    def x_start(where, carry):
        x_copy(where, xc, where).start()
        return carry

    def x_start_when_ready(where, carry):
        pl.semaphore_wait(x_ready.at[where], 1)
        return x_start(where, carry)

    def x_wait(step, carry):
        where = lax.rem(xc + step, 4)
        x_copy(where, where, where).wait()
        return carry

    lax.fori_loop(0, xc, x_start, 0)
    lax.fori_loop(xc + 1, 4, x_start_when_ready, 0)
    lax.fori_loop(1, 4, x_wait, 0)

    def x_sum(which):
        added = total[xc * 2 + which]
        for step in range(1, 4):
            added = added + x_recv[lax.rem(xc + step, 4), which].astype(F32)
        return added

    z_send[...] = x_sum(1 - zl).astype(BF16)
    z_copy = pltpu.make_async_remote_copy(
        src_ref=z_send,
        dst_ref=z_recv,
        send_sem=red_send.at[5],
        recv_sem=red_recv.at[5],
        device_id=(other_z, me),
        device_id_type=MESH,
    )
    z_copy.start()
    mine = x_sum(zl)
    z_copy.wait()
    summed = (mine + z_recv[...].astype(F32)) * scale
    gfilter[...] = summed

    def results(which, landing, parts):
        lane = pl.ds(pl.multiple_of(which * LANES, LANES), LANES)
        for i in range(3):
            spot = pl.ds(i * LANES, LANES)
            rows = landing[lane, spot].astype(F32).T
            for other, held in parts:
                held[spot, lane] = (other[spot, lane].astype(F32) * rows).astype(BF16)

    gate_leave()
    back_leave()
    conv_arrive()

    def conv_results(which, carry):
        results(which, conv_recv, [(query, out), (cotan, gquery)])
        return carry

    lax.fori_loop(0, 4, conv_results, 0)
    conv_leave()
    for dz in row_order:
        bconv_arrive(dz)
        results(lax.rem(z + 4 - dz, 4), bconv_recv, [(value, gkey), (key, gvalue)])
    bconv_leave()


def store(*refs):
    held, results, sems = refs[:5], refs[5:10], refs[10]
    copies = [
        pltpu.make_async_copy(src, dst, sems.at[index])
        for index, (src, dst) in enumerate(zip(held, results))
    ]
    for copy in copies:
        copy.start()
    for copy in copies:
        copy.wait()


def on_device(tables, query_feat, key_feat, value_feat, filter_taps, out_cotangent):
    tokens, width = query_feat.shape[1:]
    sources = lax.axis_size("ctx")
    channels = width // sources
    groups = channels // GROUP
    rows = sources * 3
    scale = 1.0 / math.sqrt(lax.axis_size("rep") * tokens * sources)
    anywhere = pl.BlockSpec(memory_space=pl.ANY)
    inside = pl.BlockSpec(memory_space=pltpu.VMEM)
    vmem = pltpu.VMEM
    features = (query_feat[0], key_feat[0], value_feat[0], out_cotangent[0])
    held = pl.pallas_call(
        functools.partial(kernel, scale, sources, channels),
        out_shape=(*[vmem((tokens, width), BF16)] * 4, vmem((channels, tokens), F32)),
        in_specs=[pl.BlockSpec(memory_space=pltpu.HBM)] * 6,
        out_specs=(inside,) * 5,
        scratch_shapes=[
            *[vmem((tokens, width), BF16)] * 4,
            vmem(filter_taps.shape[::-1], F32),
            vmem(tables.shape, F32),
            vmem((2 * HALF, 3 * rows), BF16),
            vmem((rows, 4 * HALF), BF16),
            vmem((4 * LANES, 2 * LANES), BF16),
            vmem((4 * LANES, 2 * LANES), BF16),
            vmem((2, HALF, LANES), F32),
            vmem((width, tokens), BF16),
            vmem((width, tokens), BF16),
            vmem((width, tokens), BF16),
            vmem((width, tokens), BF16),
            vmem((width, tokens), BF16),
            vmem((width, tokens), BF16),
            vmem((width, tokens), BF16),
            vmem((width, tokens), BF16),
            vmem((3, sources * channels, LANES), F32),
            vmem((3, sources * channels, LANES), F32),
            vmem((groups, GROUP * HALF, 2 * LANES), F32),
            vmem((groups, GROUP * HALF, 2 * LANES), F32),
            vmem((8, channels, tokens), BF16),
            vmem((8, channels, tokens), BF16),
            vmem((8, channels, tokens), BF16),
            vmem((4, 2, channels, tokens), BF16),
            vmem((channels, tokens), BF16),
            vmem((channels, tokens), BF16),
            vmem((8, channels, tokens), F32),
            pltpu.SemaphoreType.DMA((6,)),
            pltpu.SemaphoreType.DMA((4,)),
            pltpu.SemaphoreType.DMA((4,)),
            pltpu.SemaphoreType.DMA((3,)),
            pltpu.SemaphoreType.DMA((4,)),
            pltpu.SemaphoreType.DMA((6,)),
            pltpu.SemaphoreType.DMA((6,)),
            pltpu.SemaphoreType.REGULAR((4,)),
        ],
        compiler_params=pltpu.CompilerParams(
            collective_id=0, has_side_effects=True, vmem_limit_bytes=60 * 2**20
        ),
    )(*features, filter_taps.T, jnp.asarray(tables))
    seq = jax.ShapeDtypeStruct((tokens, width), BF16)
    outs = pl.pallas_call(
        store,
        out_shape=(seq, seq, seq, seq, jax.ShapeDtypeStruct((channels, tokens), F32)),
        in_specs=[inside] * 5,
        out_specs=(anywhere,) * 5,
        scratch_shapes=[pltpu.SemaphoreType.DMA((5,))],
        compiler_params=pltpu.CompilerParams(vmem_limit_bytes=4 * 2**20),
    )(*held)
    return (*[out[None] for out in outs[:4]], outs[4].T)


def solution(mesh):
    tables = wave_tables(mesh.shape["ctx"])
    rows = P("rep", "ctx", None)
    return jax.shard_map(
        functools.partial(on_device, tables),
        mesh=mesh,
        in_specs=(rows, rows, rows, P(None, "ctx"), rows),
        out_specs=(rows, rows, rows, rows, P("rep", "ctx")),
        check_vma=False,
    )
```
